256 devices in a mesh: replica: 32 (over x_hi, z, core), tensor: 8 (over x_lo, y).
Axes of the slice: x: 4 (x_hi: 2, x_lo: 2; x = x_hi * 2 + x_lo), y: 4, z: 8, core: 2. Of those that a mesh axis runs over, the one named last changes fastest.
Arguments:
- delta_codes: int32 [32, 2, 4096, 1024], P('replica', None, None, 'tensor'), may hold values from 0 to 255
- scale_exponents: int32 [32, 2, 256, 1024], P('replica', None, None, 'tensor'), may hold values from -5 to -1
- outer_params: float32 [2, 8192, 1024], P(None, 'replica', 'tensor'), may hold values from -6 to 6
- outer_momentum: float32 [2, 8192, 1024], P(None, 'replica', 'tensor'), may hold values from -4 to 4
- tensor_partials: bfloat16 [8, 12288, 8192], P('tensor', 'replica'), may hold values from -6 to 6
- residual_stream: bfloat16 [12288, 8192], P('replica', 'tensor'), may hold values from -150 to 150, as said below
- norm_gain: float32 [8192], replicated, may hold values from 0.1 to 1.9
Outputs:
- keys_values: bfloat16 [2, 12288, 1024], P(None, 'replica', 'tensor')
- params_out: float32 [2, 8192, 1024], P(None, 'replica', 'tensor')
- momentum_out: float32 [2, 8192, 1024], P(None, 'replica', 'tensor')
The draws below stay inside these ranges and needn't reach their ends.
Inputs may be any that keep to these rules, and one draw needn't show every extreme that they name: residual_stream has rows and features of differing scales.
All inputs are finite; a program needn't handle non-finite values.
Results may differ from the reference program's by a relative error of at most 0.018.
Values may be sent and summed in bfloat16 or wider, within the bound.
A program may use at most 128 MiB of HBM per device.

```python
import jax
import jax.numpy as jnp
from jax import lax

D = 8192
KVW = 1024
BLOCK = 32
TOKENS = 12288
N_REPLICA = 32
N_TENSOR = 8


def draw_residual_stream(key, part):
    key = jax.random.fold_in(key, 11)
    key_base, key_rows, key_columns = jax.random.split(key, 3)
    row_scale = jnp.exp(jax.random.uniform(key_rows, (TOKENS, 1), jnp.float32, jnp.log(0.5), jnp.log(5.0)))
    column_scale = jnp.exp(jax.random.uniform(key_columns, (1, D), jnp.float32, jnp.log(0.5), jnp.log(5.0)))
    base_value = jnp.clip(jax.random.normal(key_base, (TOKENS, D), jnp.float32), -6.0, 6.0)
    return (base_value * row_scale * column_scale).astype(jnp.bfloat16)


def place_ends(array, rng, least, largest):
    index_at = [jax.random.randint(jax.random.fold_in(rng, axis), (), 0, length) for axis, length in enumerate(array.shape)]
    longest = array.shape.index(max(array.shape))
    next_to = index_at[:longest] + [(index_at[longest] + 1) % array.shape[longest]] + index_at[longest + 1:]
    return array.at[tuple(index_at)].set(least).at[tuple(next_to)].set(largest)


def level_of(key, dims, cuts, low, largest):
    factor_of = 1.0
    for dim, blocks in cuts:
        draws = jax.random.uniform(jax.random.fold_in(jax.random.fold_in(key, 6), dim), (blocks,), jnp.float32, low / len(cuts), largest / len(cuts))
        factor_of = factor_of * jnp.repeat(jnp.exp(draws), dims[dim] // blocks).reshape((-1,) + (1,) * (len(dims) - 1 - dim))
    return factor_of


def centred(stream_key, dims, scale, bound, pieces=(), dtype=jnp.bfloat16):
    level = level_of(stream_key, dims, pieces, -0.22, 0.18) if pieces else 1.0
    entries = jax.random.normal(stream_key, dims, jnp.float32) * scale * level
    return jnp.minimum(jnp.maximum(entries, -bound), bound).astype(dtype)


def setup_inputs(seed: int = 0) -> dict:
    key_list = jax.random.split(jax.random.key(seed), 8)
    delta_codes = place_ends(jax.random.randint(key_list[0], (N_REPLICA, 2, D // 2, KVW), 0, 256), jax.random.fold_in(key_list[0], 1), 0, 255).astype(jnp.int32)
    scale_exponents = place_ends(jax.random.randint(key_list[1], (N_REPLICA, 2, D // BLOCK, KVW), -5, 0), jax.random.fold_in(key_list[1], 1), -5, -1).astype(jnp.int32)
    outer_params = centred(key_list[2], (2, D, KVW), 1.0, 6.0, ((1, 32), (2, 8)), jnp.float32)
    outer_momentum = centred(key_list[3], (2, D, KVW), 0.3, 4.0, ((1, 32), (2, 8)), jnp.float32)
    tensor_partials = centred(key_list[4], (N_TENSOR, TOKENS, D), 1.0, 6.0, ((0, 8), (1, 32)))
    residual_stream = draw_residual_stream(jax.random.fold_in(key_list[7], 71), 0)
    norm_gain = jnp.clip(1.0 + 0.18 * jax.random.normal(key_list[6], (D,), jnp.float32), 0.1, 1.9)
    return dict(delta_codes=delta_codes, scale_exponents=scale_exponents, outer_params=outer_params, outer_momentum=outer_momentum, tensor_partials=tensor_partials, residual_stream=residual_stream, norm_gain=norm_gain)


outer_rate = 0.7
outer_beta = 0.9
lowest_exponent = -5
norm_epsilon = 1e-05

def unpack_codes(words):
    nibbles = [jnp.bitwise_and(jnp.right_shift(words, 4 * place), 15) for place in range(2)]
    stacked = jnp.stack(nibbles, axis=2)
    return stacked.reshape(words.shape[0], words.shape[1] * 2, words.shape[2]).astype(jnp.int32)

def decode_block(words, exponents):
    codes = unpack_codes(words)
    magnitude = codes % 8
    sign_factor = 1.0 - 2.0 * (codes // 8).astype(jnp.float32)
    exponent_bits = magnitude // 2
    mantissa = (magnitude % 2).astype(jnp.float32)
    power_part = jnp.where(exponent_bits == 3, 4.0, jnp.where(exponent_bits == 2, 2.0, 1.0))
    value = jnp.where(exponent_bits == 0, 0.5 * mantissa, power_part * (1.0 + 0.5 * mantissa)) * sign_factor
    block_scale = jnp.left_shift(jnp.ones_like(exponents), exponents - lowest_exponent).astype(jnp.float32) * 2.0 ** lowest_exponent
    shaped = value.reshape(codes.shape[0], codes.shape[1] // BLOCK, BLOCK, codes.shape[2]) * block_scale[:, :, None, :]
    return shaped.reshape(codes.shape).astype(jnp.bfloat16)

def reference(delta_codes, scale_exponents, outer_params, outer_momentum, tensor_partials, residual_stream, norm_gain):

    def add_replica(summed, inputs_pair):
        return (summed + decode_block(inputs_pair[0], inputs_pair[1]).astype(jnp.float32), None)
    summed, _ = lax.scan(add_replica, jnp.zeros(outer_params.shape, jnp.float32), (delta_codes, scale_exponents))
    outer_grad = summed / N_REPLICA
    momentum_out = outer_beta * outer_momentum + outer_grad
    params_out = outer_params - outer_rate * (outer_grad + outer_beta * momentum_out)
    fragment = params_out.astype(jnp.bfloat16)

    def add_partial(running, partial_term):
        return (running + partial_term.astype(jnp.float32), None)
    hidden_sum, _ = lax.scan(add_partial, residual_stream.astype(jnp.float32), tensor_partials)
    hidden = hidden_sum.astype(jnp.bfloat16)
    hidden_float = hidden.astype(jnp.float32)
    inverse = lax.rsqrt(lax.optimization_barrier(jnp.mean(hidden_float * hidden_float, axis=-1, keepdims=True)) + norm_epsilon)
    normed = (hidden_float * inverse * norm_gain.astype(jnp.float32)).astype(jnp.bfloat16)
    projected = jnp.einsum('td,jdk->jtk', normed.astype(jnp.float32), fragment.astype(jnp.float32))
    keys_values = (projected * D ** (-0.5)).astype(jnp.bfloat16)
    return (keys_values, params_out, momentum_out)
```

```python
import jax
import jax.numpy as jnp
from jax import lax
from jax.experimental import pallas as pl
from jax.experimental.pallas import tpu as pltpu
from jax.sharding import PartitionSpec as P

D = 8192
TOK = 384
MESH = pl.DeviceIdType.MESH
F32 = jnp.float32
BF16 = jnp.bfloat16

outer_rate = 0.7
outer_beta = 0.9
norm_epsilon = 1e-05

Y_FIRST = (0, 1, 2, 3, 4)
X_FIRST = (5, 6, 7)
H_ORDER = (0, 5, 1, 2, 6, 3, 4, 7)


class Slots:
    def __init__(self):
        self.total = 0
        self.base = {}

    def add(self, name, count):
        self.base[name] = self.total
        self.total += count

    def __getitem__(self, name):
        return self.base[name]


RECV = Slots()
for _name, _count in (
    ("sib", 4), ("z", 4 * 2 * 4), ("xh", 4), ("a2a", 16), ("ag", 4 * 2 * 2), ("ya", 8 * 2), ("yb", 8 * 2),
    ("yc", 8 * 2), ("xl", 8), ("asib", 8), ("ss", 8), ("p", 16),
):
    RECV.add(_name, _count)
N_SEND = 192
LOCAL = Slots()
for _name, _count in (("codes", 4), ("part", 8), ("misc", 5), ("out", 9)):
    LOCAL.add(_name, _count)


def decode_nibble(code):
    magnitude = jnp.bitwise_and(code, 7).astype(F32)
    value = jnp.maximum(jnp.maximum(0.5 * magnitude, magnitude - 2.0), 2.0 * magnitude - 8.0)
    return jnp.where(code >= 8, -value, value)


def kernel(
    codes, exps, params, momentum, partials, residual, gain,
    kv_out, params_out, momentum_out,
    cbuf, ebuf, pbuf, mbuf, rbuf, gbuf,
    dec, sibr, zrecv, zout, fin, xout, xrecv, grad, newp, newm, frag, wbuf,
    part, yra, yrb, yrc, yout, hs, xo, xr, xr4, xs, abuf, ssacc, ssout, ssr, pout, precv, invb, kvbuf,
    ssem, rsem, lsem,
):
    r = lax.axis_index("replica")
    t = lax.axis_index("tensor")
    xh = r // 16
    z = lax.rem(r // 2, 8)
    c = lax.rem(r, 2)
    xl = t // 4
    y = lax.rem(t, 4)

    def dev(xh_, z_, c_, xl_, y_):
        return (xh_ * 16 + z_ * 2 + c_, xl_ * 4 + y_)

    def zp(n):
        return lax.rem(z + 8 + n, 8)

    def yp(n):
        return lax.rem(y + 4 + n, 4)

    sibling = dev(xh, z, 1 - c, xl, y)
    x_pair = dev(xh, z, c, 1 - xl, y)
    xh_pair = dev(1 - xh, z, c, xl, y)
    z_next = (dev(xh, zp(1), c, xl, y), dev(xh, zp(-1), c, xl, y))
    y_next = (dev(xh, z, c, xl, yp(1)), dev(xh, z, c, xl, yp(-1)))

    sends = []

    def send(src, dst, recv_index, device, cond=None):
        index = len(sends)
        copy = pltpu.make_async_remote_copy(
            src_ref=src, dst_ref=dst, send_sem=ssem.at[index], recv_sem=rsem.at[recv_index],
            device_id=device, device_id_type=MESH,
        )
        if cond is None:
            copy.start()
        else:
            @pl.when(cond)
            def _():
                copy.start()
        sends.append((copy, cond))

    def wait_recv(dst, recv_index):
        pltpu.make_async_remote_copy(
            src_ref=dst, dst_ref=dst, send_sem=ssem.at[0], recv_sem=rsem.at[recv_index],
            device_id=sibling, device_id_type=MESH,
        ).wait_recv()

    def load(src, dst, index):
        copy = pltpu.make_async_copy(src, dst, lsem.at[index])
        copy.start()
        return copy

    code_loads = [None] * 4
    part_loads = [None] * 8

    def load_codes(q):
        code_loads[q] = load(codes.at[q // 2, :, q % 2], cbuf.at[q], LOCAL["codes"] + q)

    def load_part(k):
        part_loads[k] = load(partials.at[:, pl.ds(1024 * k, 1024)], part.at[k], LOCAL["part"] + k)

    exp_load = load(exps, ebuf, LOCAL["misc"])
    load_codes(0)
    res_load = load(residual, rbuf, LOCAL["misc"] + 1)
    load_part(H_ORDER[0])
    load_part(H_ORDER[1])
    load_codes(1)
    load_part(H_ORDER[2])
    load_codes(2)
    load_codes(3)
    for k in H_ORDER[3:]:
        load_part(k)
    param_load = load(params, pbuf, LOCAL["misc"] + 2)
    momentum_load = load(momentum, mbuf, LOCAL["misc"] + 3)
    gain_load = load(gain, gbuf, LOCAL["misc"] + 4)

    barrier = pltpu.get_barrier_semaphore()
    for a in range(2):
        for b in range(2):
            for d in range(2):
                for e in range(4):
                    if a + b + d + e:
                        other = dev(
                            1 - xh if a else xh, z, 1 - c if b else c, 1 - xl if d else xl, yp(e)
                        )
                        pl.semaphore_signal(barrier, inc=1, device_id=other, device_id_type=MESH)
    for other in z_next:
        pl.semaphore_signal(barrier, inc=1, device_id=other, device_id_type=MESH)

    def decode(q, core):
        j, half = q // 2, q % 2

        @pl.loop(0, 16)
        def _(i):
            owner = i * 2 + core
            for b in range(4):
                exponent = ebuf[j, owner, pl.ds(4 * half + b, 1), :]
                scale = jnp.left_shift(jnp.ones_like(exponent), exponent + 5).astype(F32) * 2.0**-5
                words = cbuf[q, owner, pl.ds(16 * b, 16), :]
                low = decode_nibble(jnp.bitwise_and(words, 15)) * scale
                high = decode_nibble(jnp.bitwise_and(jnp.right_shift(words, 4), 15)) * scale
                dec[q, core, i // 8, lax.rem(i, 8), pl.ds(16 * b, 16), :] = low.astype(BF16)
                dec[q, core, i // 8, lax.rem(i, 8), pl.ds(64 + 16 * b, 16), :] = high.astype(BF16)

    tasks = []

    def task(time, function, *arguments):
        tasks.append((time, len(tasks), function, arguments))

    def g_decode_other(q):
        code_loads[q].wait()
        if q == 0:
            exp_load.wait()
        decode(q, 1 - c)
        if q == 0:
            pl.semaphore_wait(barrier, 33)
        send(dec.at[q, 1 - c], sibr.at[q], RECV["sib"] + q, sibling)

    def g_decode_own(q):
        decode(q, c)

    def g_pair(q):
        wait_recv(sibr.at[q], RECV["sib"] + q)

        @pl.loop(0, 16)
        def _(i):
            a, b = i // 8, lax.rem(i, 8)
            dec[q, c, a, b] = (dec[q, c, a, b].astype(F32) + sibr[q, a, b].astype(F32)).astype(BF16)

        for d in range(2):
            send(dec.at[q, c, d, zp(4)], zrecv.at[q, d, 0, d], RECV["z"] + (q * 2 + d) * 4, z_next[d])

    def g_ring(q, step):
        for d in range(2):
            sign = 1 - 2 * d
            target = zp(sign * (5 - step))
            index = RECV["z"] + (q * 2 + d) * 4 + step - 2
            if step == 2:
                wait_recv(zrecv.at[q, d, 0, d], index)
                zout[q, d, step - 2, d] = (
                    dec[q, c, d, target].astype(F32) + zrecv[q, d, 0, d].astype(F32)
                ).astype(BF16)
                zout[q, d, step - 2, 1 - d] = dec[q, c, 1 - d, target]
            else:
                wait_recv(zrecv.at[q, d, step - 2], index)
                for a in range(2):
                    zout[q, d, step - 2, a] = (
                        dec[q, c, a, target].astype(F32) + zrecv[q, d, step - 2, a].astype(F32)
                    ).astype(BF16)
            send(zout.at[q, d, step - 2], zrecv.at[q, d, step - 1], index + 1, z_next[d])

    def g_final(q):
        for d in range(2):
            wait_recv(zrecv.at[q, d, 3], RECV["z"] + (q * 2 + d) * 4 + 3)

        def total(a):
            return (
                dec[q, c, a, z].astype(F32) + zrecv[q, 0, 3, a].astype(F32) + zrecv[q, 1, 3, a].astype(F32)
            )

        xout[q] = total(1 - xh).astype(BF16)
        send(xout.at[q], xrecv.at[q], RECV["xh"] + q, xh_pair)
        fin[q] = total(xh)

    is_source = xl == lax.rem(z, 2)

    def g_update(q):
        j, half = q // 2, q % 2
        if q == 0:
            param_load.wait()
            momentum_load.wait()
        wait_recv(xrecv.at[q], RECV["xh"] + q)
        summed = fin[q] + xrecv[q].astype(F32)
        grad[q, pl.ds(0, 64, stride=2), :] = summed[:64]
        grad[q, pl.ds(1, 64, stride=2), :] = summed[64:]
        outer_grad = grad[q] * (1.0 / 32.0)
        rows = pl.ds(128 * half, 128)
        new_momentum = outer_beta * mbuf[j, rows, :] + outer_grad
        new_params = pbuf[j, rows, :] - outer_rate * (outer_grad + outer_beta * new_momentum)
        newm[j, rows, :] = new_momentum
        newp[j, rows, :] = new_params
        frag[q] = new_params.astype(BF16)
        y_to = 2 * c + half
        x_to = lax.rem(z, 2)
        column = lax.rem(y - y_to + 4 + 3, 4) * 2 + xl
        slot = wbuf.at[(z // 2) * 2 + xh, :, pl.ds(pl.multiple_of(128 * column, 128), 128)]
        index = RECV["a2a"] + xh * 8 + column
        here = (c == j) & (xl == x_to) & (y == y_to)

        @pl.when(here)
        def _():
            pltpu.make_async_copy(frag.at[q], slot, rsem.at[index]).start()

        send(frag.at[q], slot, index, dev(xh, z, j, x_to, y_to), jnp.logical_not(here))
        send(frag.at[q], slot, index, dev(1 - xh, z, j, x_to, y_to))

    def w_block(source_z, i):
        return wbuf.at[pl.ds((source_z // 2) * 2, 2), :, pl.ds(256 * i, 256)]

    def w_half(source_z, a, i):
        return wbuf.at[(source_z // 2) * 2 + a, :, pl.ds(256 * i, 256)]

    def ag_index(i, d, step):
        return RECV["ag"] + (i * 2 + d) * 2 + step

    def w_first(i):
        @pl.when(is_source)
        def _():
            for a in range(2):
                for column in (2 * i, 2 * i + 1):
                    piece = wbuf.at[(z // 2) * 2 + a, :, pl.ds(128 * column, 128)]
                    wait_recv(piece, RECV["a2a"] + a * 8 + column)

        for d in range(2):
            sign = 1 - 2 * d

            @pl.when(jnp.logical_not(is_source))
            def _():
                wait_recv(w_block(zp(-sign), i), ag_index(i, d, 0))

            origin = jnp.where(is_source, z, zp(-sign))
            send(w_block(origin, i), w_block(origin, i), ag_index(i, d, 0), z_next[d])

    def w_second(i):
        for d in range(2):
            sign = 1 - 2 * d

            @pl.when(is_source)
            def _():
                wait_recv(w_block(zp(-2 * sign), i), ag_index(i, d, 0))

            @pl.when(jnp.logical_not(is_source))
            def _():
                wait_recv(w_block(zp(-3 * sign), i), ag_index(i, d, 1))

            block = w_block(zp(-2 * sign), i)
            send(block, block, ag_index(i, d, 1), z_next[d], is_source)
            piece = w_half(zp(-3 * sign), d, i)
            send(piece, piece, ag_index(i, d, 1), z_next[d], jnp.logical_not(is_source))

    def w_last(i):
        @pl.when(is_source)
        def _():
            for d in range(2):
                wait_recv(w_half(zp(4), d, i), ag_index(i, d, 1))

    def lanes(x_, y_):
        return pl.ds(pl.multiple_of(128 * (x_ * 4 + y_), 128), 128)

    def add_rows(out, rows, *terms):
        @pl.loop(0, rows // 64)
        def _(i):
            at = pl.ds(pl.multiple_of(i * 64, 64), 64)
            value = terms[0](at).astype(F32)
            for term in terms[1:]:
                value = value + term(at).astype(F32)
            out(at, value)

    def h_load(k):
        part_loads[k].wait()
        if k == H_ORDER[0]:
            res_load.wait()

        @pl.when(t == k)
        def _():
            @pl.loop(0, TOK // 16)
            def _(i):
                at = pl.ds(pl.multiple_of(i * 16, 16), 16)
                part[k, at, :] = (part[k, at, :].astype(F32) + rbuf[at, :].astype(F32)).astype(BF16)

    def hy_start(k):
        h_load(k)
        n = Y_FIRST.index(k)
        for d in range(2):
            sign = 1 - 2 * d
            send(part.at[k, :, lanes(d, yp(2))], yra.at[n, d], RECV["ya"] + k * 2 + d, y_next[d])
        for d in range(2):
            sign = 1 - 2 * d
            send(part.at[k, :, lanes(1 - d, yp(sign))], yrb.at[n, d], RECV["yb"] + k * 2 + d, y_next[d])

    def hy_middle(k):
        n = Y_FIRST.index(k)
        for d in range(2):
            sign = 1 - 2 * d
            wait_recv(yra.at[n, d], RECV["ya"] + k * 2 + d)
            own = lanes(d, yp(sign))

            def put(at, value, d=d):
                yout[n, d, at, :] = value.astype(BF16)

            add_rows(put, TOK, lambda at, own=own: part[k, at, own], lambda at, d=d: yra[n, d, at, :])
            send(yout.at[n, d], yrc.at[n, d], RECV["yc"] + k * 2 + d, y_next[d])

    def hy_cross(k):
        n = Y_FIRST.index(k)
        for d in range(2):
            wait_recv(yrb.at[n, d], RECV["yb"] + k * 2 + d)
            wait_recv(yrc.at[n, d], RECV["yc"] + k * 2 + d)

        def put_other(at, value):
            xo[n, at, :] = value.astype(BF16)

        def put_own(at, value):
            hs[n, at, :] = value

        for x_, put in ((1 - xl, put_other), (xl, put_own)):
            own = lanes(x_, y)
            add_rows(
                put, TOK, lambda at, own=own: part[k, at, own], lambda at, x_=x_: yrb[n, 1 - x_, at, :],
                lambda at, x_=x_: yrc[n, x_, at, :],
            )
            if put is put_other:
                send(xo.at[n], xr.at[n], RECV["xl"] + k, x_pair)

    first_done = []

    def finish(k, at, value):
        hidden = value.astype(BF16).astype(F32)
        position = (k % 4) * 2 + k // 4
        scaled = hidden * gbuf[pl.ds(8 * k + t, 1), :]
        abuf[c, at, pl.ds(128 * position, 128)] = scaled.astype(BF16)
        if first_done:
            ssacc[at, :] += hidden * hidden
        else:
            ssacc[at, :] = hidden * hidden

    def finished(k):
        first_done.append(k)
        position = (k % 4) * 2 + k // 4
        piece = abuf.at[c, :, pl.ds(128 * position, 128)]
        send(piece, piece, RECV["asib"] + k, sibling)

    def hy_end(k):
        n = Y_FIRST.index(k)
        if not first_done:
            gain_load.wait()
        wait_recv(xr.at[n], RECV["xl"] + k)
        add_rows(
            lambda at, value: finish(k, at, value), TOK, lambda at: hs[n, at, :], lambda at: xr[n, at, :]
        )
        finished(k)

    def hx_start(k):
        h_load(k)
        n = X_FIRST.index(k)
        other = pl.ds(pl.multiple_of(512 * (1 - xl), 512), 512)
        send(part.at[k, :, other], xr4.at[n], RECV["xl"] + k, x_pair)

    half_rows = (pl.ds(0, 192), pl.ds(192, 192))

    def hx_lanes(y_):
        return pl.ds(pl.multiple_of(128 * y_, 128), 128)

    def hx_cross(k):
        n = X_FIRST.index(k)
        wait_recv(xr4.at[n], RECV["xl"] + k)
        own = pl.ds(pl.multiple_of(512 * xl, 512), 512)

        @pl.loop(0, TOK // 16)
        def _(i):
            at = pl.ds(pl.multiple_of(i * 16, 16), 16)
            xs[n, at, :] = (part[k, at, own].astype(F32) + xr4[n, at, :].astype(F32)).astype(BF16)

        for d in range(2):
            send(
                xs.at[n, half_rows[d], hx_lanes(yp(2))], yra.at[len(Y_FIRST) + n, d, pl.ds(0, 192)],
                RECV["ya"] + k * 2 + d, y_next[d],
            )

    def hx_middle(k):
        n = X_FIRST.index(k)
        m = len(Y_FIRST) + n
        for d in range(2):
            sign = 1 - 2 * d
            wait_recv(yra.at[m, d, pl.ds(0, 192)], RECV["ya"] + k * 2 + d)
            own = hx_lanes(yp(sign))

            @pl.loop(0, 192 // 64)
            def _(i, d=d, own=own):
                at = pl.ds(pl.multiple_of(192 * d + i * 64, 64), 64)
                got = pl.ds(pl.multiple_of(i * 64, 64), 64)
                xs[n, at, own] = (xs[n, at, own].astype(F32) + yra[m, d, got, :].astype(F32)).astype(BF16)

            send(xs.at[n, :, own], yrc.at[m, d], RECV["yc"] + k * 2 + d, y_next[d])

    def hx_end(k):
        n = X_FIRST.index(k)
        m = len(Y_FIRST) + n
        if not first_done:
            gain_load.wait()
        for d in range(2):
            wait_recv(yrc.at[m, d], RECV["yc"] + k * 2 + d)
        own = hx_lanes(y)
        add_rows(
            lambda at, value: finish(k, at, value), TOK, lambda at: xs[n, at, own],
            lambda at: yrc[m, 0, at, :], lambda at: yrc[m, 1, at, :],
        )
        finished(k)

    def ss_send():
        for b in range(3):
            block = jnp.sum(ssacc[pl.ds(128 * b, 128), :].T, axis=0, keepdims=True)
            ssout[:, pl.ds(128 * b, 128)] = jnp.broadcast_to(block, (8, 128))
        ssr[t] = ssout[...]
        for d in range(2):
            for e in range(4):
                if d + e:
                    device = dev(xh, z, c, 1 - xl if d else xl, yp(e))
                    send(ssout, ssr.at[t], RECV["ss"] + t, device)

    def ss_receive():
        total = ssr[t]
        for d in range(2):
            for e in range(4):
                if d + e:
                    source = (1 - xl if d else xl) * 4 + yp(e)
                    wait_recv(ssr.at[source], RECV["ss"] + source)
        total = ssr[0]
        for source in range(1, 8):
            total = total + ssr[source]
        inverse = lax.rsqrt(total * (1.0 / D) + norm_epsilon) * D**-0.5
        for b in range(3):
            block = jnp.broadcast_to(inverse[0:1, 128 * b : 128 * b + 128], (128, 128))
            invb[pl.ds(128 * b, 128), :] = block.T

    def project(i):
        if i == 0:
            for k in range(8):
                position = (k % 4) * 2 + k // 4
                wait_recv(abuf.at[1 - c, :, pl.ds(128 * position, 128)], RECV["asib"] + k)
        w = wbuf[:, :, pl.ds(256 * i, 256)].reshape(1024, 256)
        y_to = yp(1 + i)
        for b in range(2):
            pout[i, b] = jnp.dot(abuf[b], w, preferred_element_type=F32).astype(BF16)
            for x_to in range(2):
                piece = pout.at[i, b, :, pl.ds(128 * x_to, 128)]
                slot = precv.at[c, t]
                index = RECV["p"] + c * 8 + t
                device = dev(xh, z, b, x_to, y_to)
                if i < 3:
                    send(piece, slot, index, device)
                else:
                    here = (c == b) & (xl == x_to)

                    @pl.when(here)
                    def _():
                        pltpu.make_async_copy(piece, slot, rsem.at[index]).start()

                    send(piece, slot, index, device, jnp.logical_not(here))

    def result():
        for j in range(2):
            for source in range(8):
                wait_recv(precv.at[j, source], RECV["p"] + j * 8 + source)

            @pl.loop(0, TOK // 32)
            def _(i):
                at = pl.ds(pl.multiple_of(i * 32, 32), 32)
                value = precv[j, 0, at, :].astype(F32)
                for source in range(1, 8):
                    value = value + precv[j, source, at, :].astype(F32)
                kvbuf[j, at, :] = (value * invb[at, :]).astype(BF16)

    starts = (0.0, 1.0, 5.0, 6.0)
    for q in range(4):
        task(0.0 + 1.2 * q, g_decode_other, q)
        task(0.6 + 1.2 * q, g_decode_own, q)
        task(4.5 + starts[q], g_pair, q)
        for step in (2, 3, 4):
            task(4.5 + starts[q] + 4.0 * (step - 1), g_ring, q, step)
        task(20.5 + starts[q], g_final, q)
        task(24.5 + starts[q], g_update, q)
    for i in range(4):
        task(36.0 + 2.0 * i, w_first, i)
        task(44.0 + 3.0 * i, w_second, i)
        task(55.0 + 3.0 * i, w_last, i)
        task(55.1 + 3.0 * i, project, i)
    for n, k in enumerate(H_ORDER):
        start = 0.3 + 1.5 * n if n < 3 else 4.0 + 5.0 * (n - 2)
        if k in Y_FIRST:
            task(start, hy_start, k)
            task(start + 7.0, hy_middle, k)
            task(start + 14.0, hy_cross, k)
            task(start + 19.0, hy_end, k)
        else:
            task(start, hx_start, k)
            task(start + 10.0, hx_cross, k)
            task(start + 15.0, hx_middle, k)
            task(start + 20.0, hx_end, k)
    task(52.0, ss_send)
    task(64.3, ss_receive)
    task(70.0, result)
    outs = []
    for _, _, function, arguments in sorted(tasks, key=lambda item: item[:2]):
        function(*arguments)
        if function is g_update and arguments == (3,):
            outs.append(load(newp, params_out, LOCAL["out"]))
            outs.append(load(newm, momentum_out, LOCAL["out"] + 1))
    outs.append(load(kvbuf, kv_out, LOCAL["out"] + 2))
    for copy, cond in sends:
        if cond is None:
            copy.wait_send()
        else:
            @pl.when(cond)
            def _():
                copy.wait_send()
    for copy in outs:
        copy.wait()


def per_device(
    delta_codes, scale_exponents, outer_params, outer_momentum, tensor_partials, residual_stream, norm_gain
):
    ny, nx = len(Y_FIRST), len(X_FIRST)
    vmem = pltpu.VMEM
    scratch = [
        vmem((4, 32, 64, 128), jnp.int32),
        vmem((2, 32, 8, 128), jnp.int32),
        vmem((2, 256, 128), F32),
        vmem((2, 256, 128), F32),
        vmem((TOK, 1024), BF16),
        vmem((64, 128), F32),
        vmem((4, 2, 2, 8, 128, 128), BF16),
        vmem((4, 2, 8, 128, 128), BF16),
        vmem((4, 2, 4, 2, 128, 128), BF16),
        vmem((4, 2, 3, 2, 128, 128), BF16),
        vmem((4, 128, 128), F32),
        vmem((4, 128, 128), BF16),
        vmem((4, 128, 128), BF16),
        vmem((4, 128, 128), F32),
        vmem((2, 256, 128), F32),
        vmem((2, 256, 128), F32),
        vmem((4, 128, 128), BF16),
        vmem((8, 128, 1024), BF16),
        vmem((8, TOK, 1024), BF16),
        vmem((8, 2, TOK, 128), BF16),
        vmem((ny, 2, TOK, 128), BF16),
        vmem((8, 2, TOK, 128), BF16),
        vmem((ny, 2, TOK, 128), BF16),
        vmem((ny, TOK, 128), F32),
        vmem((ny, TOK, 128), BF16),
        vmem((ny, TOK, 128), BF16),
        vmem((nx, TOK, 512), BF16),
        vmem((nx, TOK, 512), BF16),
        vmem((2, TOK, 1024), BF16),
        vmem((TOK, 128), F32),
        vmem((8, TOK), F32),
        vmem((8, 8, TOK), F32),
        vmem((4, 2, TOK, 256), BF16),
        vmem((2, 8, TOK, 128), BF16),
        vmem((TOK, 128), F32),
        vmem((2, TOK, 128), BF16),
        pltpu.SemaphoreType.DMA((N_SEND,)),
        pltpu.SemaphoreType.DMA((RECV.total,)),
        pltpu.SemaphoreType.DMA((LOCAL.total,)),
    ]
    any_spec = pl.BlockSpec(memory_space=pl.ANY)
    return pl.pallas_call(
        kernel,
        out_shape=(
            jax.ShapeDtypeStruct((2, TOK, 128), BF16),
            jax.ShapeDtypeStruct((2, 256, 128), F32),
            jax.ShapeDtypeStruct((2, 256, 128), F32),
        ),
        in_specs=[any_spec] * 7,
        out_specs=(any_spec,) * 3,
        scratch_shapes=scratch,
        compiler_params=pltpu.CompilerParams(
            collective_id=0, has_side_effects=True, vmem_limit_bytes=60 * 2**20
        ),
        cost_estimate=pl.CostEstimate(flops=2 * 768 * 1024 * 1024, bytes_accessed=13 * 2**20, transcendentals=0),
        name="outer_step",
    )(
        delta_codes.reshape(2, 32, 2, 64, 128),
        scale_exponents.reshape(2, 32, 8, 128),
        outer_params,
        outer_momentum,
        tensor_partials.reshape(TOK, D),
        residual_stream,
        norm_gain.reshape(64, 128),
    )


def solution(mesh):
    return jax.shard_map(
        per_device,
        mesh=mesh,
        in_specs=(
            P("replica", None, None, "tensor"),
            P("replica", None, None, "tensor"),
            P(None, "replica", "tensor"),
            P(None, "replica", "tensor"),
            P("tensor", "replica", None),
            P("replica", "tensor"),
            P(),
        ),
        out_specs=(
            P(None, "replica", "tensor"),
            P(None, "replica", "tensor"),
            P(None, "replica", "tensor"),
        ),
        check_vma=False,
    )
```

```python
import jax
import jax.numpy as jnp
from jax import lax
from jax.experimental import pallas as pl
from jax.experimental.pallas import tpu as pltpu
from jax.sharding import PartitionSpec as P

D = 8192
TOK = 384
MESH = pl.DeviceIdType.MESH
F32 = jnp.float32
BF16 = jnp.bfloat16

outer_rate = 0.7
outer_beta = 0.9
norm_epsilon = 1e-05

Y_FIRST = (0, 1, 2, 3, 4, 5, 6)
X_FIRST = (7,)
H_ORDER = (0, 7, 1, 2, 3, 4, 5, 6)


PLAN = {
    "other": (1.5, 3.7, 6.8, 10.0),
    "own": (3.0, 5.4, 7.5, 10.7),
    "pair": (4.9, 6.3, 9.6, 13.0),
    "hop": 3.5,
    "cross": 4.0,
    "gather": (29.0, 37.0),
    "piece": 0.8,
    "relay": 4.0,
    "start": (3.1, 3.2, 5.5, 10.5, 15.0, 19.0, 24.0, 29.0),
    "y": (0.0, 7.0, 14.0, 19.0),
    "x": (0.0, 10.0, 15.0, 20.0, 24.0),
    "greet": (6.0, 9.0, 12.0, 14.0),
    "squares": 8.0,
}


class Slots:
    def __init__(self):
        self.total = 0
        self.base = {}

    def add(self, name, count):
        self.base[name] = self.total
        self.total += count

    def __getitem__(self, name):
        return self.base[name]


RECV = Slots()
for _name, _count in (
    ("sib", 4), ("z", 4 * 2 * 4), ("xh", 4), ("a2a", 8), ("ag", 4 * 2 * 4), ("ya", 8 * 2), ("yb", 8 * 2),
    ("yc", 8 * 2), ("xl", 8 * 2), ("asib", 8 * 2), ("ss", 4), ("p", 8),
):
    RECV.add(_name, _count)
N_SEND = 256
LOCAL = Slots()
for _name, _count in (("codes", 4), ("part", 8), ("misc", 5), ("out", 9)):
    LOCAL.add(_name, _count)


def decode_nibble(code):
    magnitude = jnp.bitwise_and(code, 7).astype(F32)
    value = jnp.maximum(jnp.maximum(0.5 * magnitude, magnitude - 2.0), 2.0 * magnitude - 8.0)
    return jnp.where(code >= 8, -value, value)


def kernel(
    codes, exps, params, momentum, partials, residual, gain,
    kv_out, params_out, momentum_out,
    cbuf, ebuf, pbuf, mbuf, rbuf, gbuf,
    dec, sibr, zrecv, zout, fin, xout, xrecv, grad, newp, newm, frag, wbuf,
    part, yra, yrb, yrc, yout, xo, xr, xr4, xs, abuf, ssacc, ssout, ssr, pout, precv, invb, kvbuf,
    ssem, rsem, lsem, plane,
):
    r = lax.axis_index("replica")
    t = lax.axis_index("tensor")
    xh = r // 16
    z = lax.rem(r // 2, 8)
    c = lax.rem(r, 2)
    xl = t // 4
    y = lax.rem(t, 4)

    def dev(xh_, z_, c_, xl_, y_):
        return (xh_ * 16 + z_ * 2 + c_, xl_ * 4 + y_)

    def zp(n):
        return lax.rem(z + 8 + n, 8)

    def yp(n):
        return lax.rem(y + 4 + n, 4)

    sibling = dev(xh, z, 1 - c, xl, y)
    x_pair = dev(xh, z, c, 1 - xl, y)
    x_cross = dev(1 - xh, z, c, 1 - xl, y)
    xh_pair = dev(1 - xh, z, c, xl, y)
    z_next = (dev(xh, zp(1), c, xl, y), dev(xh, zp(-1), c, xl, y))
    y_next = (dev(xh, z, c, xl, yp(1)), dev(xh, z, c, xl, yp(-1)))

    sends = []

    def send(src, dst, recv_index, device, cond=None, inside=None, like=None):
        index = len(sends)
        copy = pltpu.make_async_remote_copy(
            src_ref=src, dst_ref=dst, send_sem=ssem.at[index], recv_sem=rsem.at[recv_index],
            device_id=device, device_id_type=MESH,
        )
        if cond is None:
            copy.start()
        else:
            pl.when(cond)(copy.start)
        sends.append((src if like is None else like, cond if inside is None else inside))

    def wait_send(index):
        like, cond = sends[index]
        copy = pltpu.make_async_remote_copy(
            src_ref=like, dst_ref=like, send_sem=ssem.at[index], recv_sem=rsem.at[0],
            device_id=sibling, device_id_type=MESH,
        )
        if cond is None:
            copy.wait_send()
        else:
            pl.when(cond)(copy.wait_send)

    def wait_recv(dst, recv_index):
        pltpu.make_async_remote_copy(
            src_ref=dst, dst_ref=dst, send_sem=ssem.at[0], recv_sem=rsem.at[recv_index],
            device_id=sibling, device_id_type=MESH,
        ).wait_recv()

    def load(src, dst, index):
        copy = pltpu.make_async_copy(src, dst, lsem.at[index])
        copy.start()
        return copy

    code_loads = [None] * 4
    part_loads = [None] * 8

    def load_codes(q):
        code_loads[q] = load(codes.at[q // 2, :, q % 2], cbuf.at[q], LOCAL["codes"] + q)

    def load_part(k):
        part_loads[k] = load(partials.at[:, pl.ds(1024 * k, 1024)], part.at[k], LOCAL["part"] + k)

    load_codes(0)
    exp_load = load(exps, ebuf, LOCAL["misc"])
    res_load = load(residual, rbuf, LOCAL["misc"] + 1)
    load_part(H_ORDER[0])
    state_loads = []

    def more_loads():
        load_part(H_ORDER[1])
        load_codes(1)
        load_part(H_ORDER[2])
        load_codes(2)
        load_codes(3)
        for k in H_ORDER[3:]:
            load_part(k)
        state_loads.append(load(gain, gbuf, LOCAL["misc"] + 4))
        state_loads.append(load(params, pbuf, LOCAL["misc"] + 2))
        state_loads.append(load(momentum, mbuf, LOCAL["misc"] + 3))

    barrier = pltpu.get_barrier_semaphore()
    for other in (sibling, x_pair, x_cross) + y_next + z_next:
        pl.semaphore_signal(barrier, inc=1, device_id=other, device_id_type=MESH)

    def greet(stage):
        others = (y_next, (x_pair, x_cross), (x_pair, x_cross), (sibling,))
        if stage:
            pl.semaphore_wait(plane.at[stage - 1], len(others[stage - 1]))
        if stage < 4:
            for other in others[stage]:
                pl.semaphore_signal(plane.at[stage], inc=1, device_id=other, device_id_type=MESH)

    def decode(q, core):
        j, half = q // 2, q % 2

        @pl.loop(0, 16)
        def _(i):
            owner = i * 2 + core
            for b in range(4):
                exponent = ebuf[j, owner, pl.ds(4 * half + b, 1), :]
                scale = jnp.left_shift(jnp.ones_like(exponent), exponent + 5).astype(F32) * 2.0**-5
                words = cbuf[q, owner, pl.ds(16 * b, 16), :]
                low = decode_nibble(jnp.bitwise_and(words, 15)) * scale
                high = decode_nibble(jnp.bitwise_and(jnp.right_shift(words, 4), 15)) * scale
                dec[q, core, i // 8, lax.rem(i, 8), pl.ds(16 * b, 16), :] = low.astype(BF16)
                dec[q, core, i // 8, lax.rem(i, 8), pl.ds(64 + 16 * b, 16), :] = high.astype(BF16)

    tasks = []

    def task(time, function, *arguments):
        tasks.append((time, len(tasks), function, arguments))

    def g_decode_other(q):
        code_loads[q].wait()
        if q == 0:
            exp_load.wait()
        decode(q, 1 - c)
        if q == 0:
            pl.semaphore_wait(barrier, 7)
            greet(0)
            more_loads()
        send(dec.at[q, 1 - c], sibr.at[q], RECV["sib"] + q, sibling)

    def g_decode_own(q):
        decode(q, c)

    def g_pair(q):
        wait_recv(sibr.at[q], RECV["sib"] + q)

        @pl.loop(0, 16)
        def _(i):
            a, b = i // 8, lax.rem(i, 8)
            dec[q, c, a, b] = (dec[q, c, a, b].astype(F32) + sibr[q, a, b].astype(F32)).astype(BF16)

        for d in range(2):
            send(dec.at[q, c, d, zp(4)], zrecv.at[q, d, 0, d], RECV["z"] + (q * 2 + d) * 4, z_next[d])

    def g_ring(q, step):
        for d in range(2):
            sign = 1 - 2 * d
            target = zp(sign * (5 - step))
            index = RECV["z"] + (q * 2 + d) * 4 + step - 2
            if step == 2:
                wait_recv(zrecv.at[q, d, 0, d], index)
                zout[q, d, step - 2, d] = (
                    dec[q, c, d, target].astype(F32) + zrecv[q, d, 0, d].astype(F32)
                ).astype(BF16)
                zout[q, d, step - 2, 1 - d] = dec[q, c, 1 - d, target]
            else:
                wait_recv(zrecv.at[q, d, step - 2], index)
                for a in range(2):
                    zout[q, d, step - 2, a] = (
                        dec[q, c, a, target].astype(F32) + zrecv[q, d, step - 2, a].astype(F32)
                    ).astype(BF16)
            send(zout.at[q, d, step - 2], zrecv.at[q, d, step - 1], index + 1, z_next[d])

    def g_final(q):
        for d in range(2):
            wait_recv(zrecv.at[q, d, 3], RECV["z"] + (q * 2 + d) * 4 + 3)

        def total(a):
            return (
                dec[q, c, a, z].astype(F32) + zrecv[q, 0, 3, a].astype(F32) + zrecv[q, 1, 3, a].astype(F32)
            )

        xout[q] = total(1 - xh).astype(BF16)
        send(xout.at[q], xrecv.at[q], RECV["xh"] + q, xh_pair)
        fin[q] = total(xh)

    away = (2, 1, 3, 0)

    def place_of(delta):
        return jnp.where(delta == 2, 0, jnp.where(delta == 1, 1, jnp.where(delta == 3, 2, 3)))

    def g_update(q):
        j, half = q // 2, q % 2
        if q == 0:
            state_loads[1].wait()
            state_loads[2].wait()
        wait_recv(xrecv.at[q], RECV["xh"] + q)
        summed = fin[q] + xrecv[q].astype(F32)
        grad[q, pl.ds(0, 64, stride=2), :] = summed[:64]
        grad[q, pl.ds(1, 64, stride=2), :] = summed[64:]
        outer_grad = grad[q] * (1.0 / 32.0)
        rows = pl.ds(128 * half, 128)
        new_momentum = outer_beta * mbuf[j, rows, :] + outer_grad
        new_params = pbuf[j, rows, :] - outer_rate * (outer_grad + outer_beta * new_momentum)
        newm[j, rows, :] = new_momentum
        newp[j, rows, :] = new_params
        frag[q] = new_params.astype(BF16)
        y_to = 2 * c + half
        column = place_of(lax.rem(y - y_to + 4, 4))
        slot = wbuf.at[z * 2 + xh, :, pl.ds(pl.multiple_of(128 * column, 128), 128)]
        index = RECV["a2a"] + xh * 4 + column
        here = (c == j) & (y == y_to)

        @pl.when(here)
        def _():
            pltpu.make_async_copy(frag.at[q], slot, rsem.at[index]).start()

        send(frag.at[q], slot, index, dev(xh, z, j, xl, y_to), jnp.logical_not(here))
        send(frag.at[q], slot, index, dev(1 - xh, z, j, xl, y_to))

    def w_block(source_z, i):
        return wbuf.at[pl.ds(source_z * 2, 2), :, pl.ds(128 * i, 128)]

    def w_half(source_z, a, i):
        return wbuf.at[source_z * 2 + a, :, pl.ds(128 * i, 128)]

    def w_step(i, core, step):
        like = w_block(0, i) if step < 3 else w_half(0, 0, i)
        mine = c == core

        @pl.when(mine)
        def _():
            if step == 0:
                for a in range(2):
                    wait_recv(w_half(z, a, i), RECV["a2a"] + a * 4 + i)
            for d in range(2):
                index = RECV["ag"] + (i * 2 + d) * 4 + step
                origin = zp((2 * d - 1) * step)
                if 0 < step < 4:
                    wait_recv(w_block(origin, i), index - 1)
                if step < 3:
                    send(w_block(origin, i), w_block(origin, i), index, z_next[d], inside=mine, like=like)
                elif step == 3:
                    piece = w_half(origin, d, i)
                    send(piece, piece, index, z_next[d], inside=mine, like=like)
                else:
                    wait_recv(w_half(origin, d, i), index - 1)

    def lanes(x_, y_):
        return pl.ds(pl.multiple_of(128 * (x_ * 4 + y_), 128), 128)

    def add_rows(out, rows, *terms):
        @pl.loop(0, rows // 64)
        def _(i):
            at = pl.ds(pl.multiple_of(i * 64, 64), 64)
            value = terms[0](at).astype(F32)
            for term in terms[1:]:
                value = value + term(at).astype(F32)
            out(at, value)

    def h_load(k):
        part_loads[k].wait()
        if k == H_ORDER[0]:
            res_load.wait()

        @pl.when(t == k)
        def _():
            @pl.loop(0, TOK // 16)
            def _(i):
                at = pl.ds(pl.multiple_of(i * 16, 16), 16)
                part[k, at, :] = (part[k, at, :].astype(F32) + rbuf[at, :].astype(F32)).astype(BF16)

    def hy_start(k):
        h_load(k)
        n = Y_FIRST.index(k)
        for d in range(2):
            sign = 1 - 2 * d
            send(part.at[k, :, lanes(d, yp(2))], yra.at[n, d], RECV["ya"] + k * 2 + d, y_next[d])
        for d in range(2):
            sign = 1 - 2 * d
            send(part.at[k, :, lanes(1 - d, yp(sign))], yrb.at[n, d], RECV["yb"] + k * 2 + d, y_next[d])

    def hy_middle(k):
        n = Y_FIRST.index(k)
        for d in range(2):
            sign = 1 - 2 * d
            wait_recv(yra.at[n, d], RECV["ya"] + k * 2 + d)
            own = lanes(d, yp(sign))

            def put(at, value, d=d):
                yout[n, d, at, :] = value.astype(BF16)

            add_rows(put, TOK, lambda at, own=own: part[k, at, own], lambda at, d=d: yra[n, d, at, :])
            send(yout.at[n, d], yrc.at[n, d], RECV["yc"] + k * 2 + d, y_next[d])

    def hy_cross(k):
        n = Y_FIRST.index(k)
        for d in range(2):
            wait_recv(yrb.at[n, d], RECV["yb"] + k * 2 + d)
            wait_recv(yrc.at[n, d], RECV["yc"] + k * 2 + d)

        for x_ in range(2):
            own = lanes(x_, y)

            def put(at, value, x_=x_):
                xo[n, x_, at, :] = value.astype(BF16)

            add_rows(
                put, TOK, lambda at, own=own: part[k, at, own], lambda at, x_=x_: yrb[n, 1 - x_, at, :],
                lambda at, x_=x_: yrc[n, x_, at, :],
            )
            send(xo.at[n, x_], xr.at[n, x_], RECV["xl"] + k * 2 + x_, x_pair)

    def place_at(k, x_):
        return pl.ds(pl.multiple_of(128 * (((2 * k) % 8) * 2 + 2 * x_ + k // 4), 128), 128)

    def finish(k, x_, at, value):
        hidden = value.astype(BF16).astype(F32)
        scaled = hidden * gbuf[pl.ds(8 * k + 4 * x_ + y, 1), :]
        abuf[c, at, place_at(k, x_)] = scaled.astype(BF16)
        ssacc[at, :] += hidden * hidden

    def finished(k, x_):
        piece = abuf.at[c, :, place_at(k, x_)]
        send(piece, piece, RECV["asib"] + k * 2 + x_, sibling)

    gain_waited = []

    def gain_ready():
        if not gain_waited:
            state_loads[0].wait()
            ssacc[...] = jnp.zeros_like(ssacc)
            gain_waited.append(True)

    def hy_end(k):
        n = Y_FIRST.index(k)
        gain_ready()
        for x_ in range(2):
            wait_recv(xr.at[n, x_], RECV["xl"] + k * 2 + x_)
            add_rows(
                lambda at, value, x_=x_: finish(k, x_, at, value), TOK,
                lambda at, x_=x_: xo[n, x_, at, :], lambda at, x_=x_: xr[n, x_, at, :],
            )
            finished(k, x_)

    def hx_start(k):
        h_load(k)
        n = X_FIRST.index(k)
        other = pl.ds(pl.multiple_of(512 * (1 - xl), 512), 512)
        send(part.at[k, :, other], xr4.at[n], RECV["xl"] + k * 2, x_pair)

    half_rows = (pl.ds(0, 192), pl.ds(192, 192))

    def hx_lanes(y_):
        return pl.ds(pl.multiple_of(128 * y_, 128), 128)

    def hx_cross(k):
        n = X_FIRST.index(k)
        wait_recv(xr4.at[n], RECV["xl"] + k * 2)
        own = pl.ds(pl.multiple_of(512 * xl, 512), 512)

        @pl.loop(0, TOK // 16)
        def _(i):
            at = pl.ds(pl.multiple_of(i * 16, 16), 16)
            xs[n, at, :] = (part[k, at, own].astype(F32) + xr4[n, at, :].astype(F32)).astype(BF16)

        for d in range(2):
            send(
                xs.at[n, half_rows[d], hx_lanes(yp(2))], yra.at[len(Y_FIRST) + n, d, pl.ds(0, 192)],
                RECV["ya"] + k * 2 + d, y_next[d],
            )

    def hx_middle(k):
        n = X_FIRST.index(k)
        m = len(Y_FIRST) + n
        for d in range(2):
            sign = 1 - 2 * d
            wait_recv(yra.at[m, d, pl.ds(0, 192)], RECV["ya"] + k * 2 + d)
            own = hx_lanes(yp(sign))

            @pl.loop(0, 192 // 64)
            def _(i, d=d, own=own):
                at = pl.ds(pl.multiple_of(192 * d + i * 64, 64), 64)
                got = pl.ds(pl.multiple_of(i * 64, 64), 64)
                xs[n, at, own] = (xs[n, at, own].astype(F32) + yra[m, d, got, :].astype(F32)).astype(BF16)

            send(xs.at[n, :, own], yrc.at[m, d], RECV["yc"] + k * 2 + d, y_next[d])

    def hx_end(k):
        n = X_FIRST.index(k)
        m = len(Y_FIRST) + n
        gain_ready()
        for d in range(2):
            wait_recv(yrc.at[m, d], RECV["yc"] + k * 2 + d)
        own = hx_lanes(y)

        def put(at, value):
            xo[m, 0, at, :] = value.astype(BF16)
            finish(k, xl, at, value)

        add_rows(
            put, TOK, lambda at: xs[n, at, own], lambda at: yrc[m, 0, at, :], lambda at: yrc[m, 1, at, :]
        )
        send(xo.at[m, 0], xr.at[m, 0], RECV["xl"] + k * 2 + 1, x_pair)
        finished(k, xl)

    def hx_last(k):
        m = len(Y_FIRST) + X_FIRST.index(k)
        wait_recv(xr.at[m, 0], RECV["xl"] + k * 2 + 1)
        add_rows(lambda at, value: finish(k, 1 - xl, at, value), TOK, lambda at: xr[m, 0, at, :])
        finished(k, 1 - xl)

    def ss_send():
        for b in range(3):
            block = jnp.sum(ssacc[pl.ds(128 * b, 128), :].T, axis=0, keepdims=True)
            ssout[:, pl.ds(128 * b, 128)] = jnp.broadcast_to(block, (8, 128))
        ssr[y] = ssout[...]
        for e in range(1, 4):
            send(ssout, ssr.at[y], RECV["ss"] + y, dev(xh, z, c, xl, yp(e)))

    def ss_receive():
        for e in range(1, 4):
            wait_recv(ssr.at[yp(e)], RECV["ss"] + yp(e))
        total = ssr[0] + ssr[1] + ssr[2] + ssr[3]
        inverse = lax.rsqrt(total * (1.0 / D) + norm_epsilon) * D**-0.5
        for b in range(3):
            block = jnp.broadcast_to(inverse[0:1, 128 * b : 128 * b + 128], (128, 128))
            invb[pl.ds(128 * b, 128), :] = block.T

    def hidden_ready():
        for k in range(8):
            for x_ in range(2):
                wait_recv(abuf.at[1 - c, :, place_at(k, x_)], RECV["asib"] + k * 2 + x_)

    pout_like = pout.at[0, 0]

    def project(i, core):
        mine = c == core

        @pl.when(mine)
        def _():
            w = wbuf[:, :, pl.ds(128 * i, 128)].reshape(2048, 128)
            for b in range(2):
                pout[i, b] = jnp.dot(abuf[b], w, preferred_element_type=F32).astype(BF16)
                slot = precv.at[core, y]
                index = RECV["p"] + core * 4 + y
                if away[i] == 0 and b == core:
                    pltpu.make_async_copy(pout.at[i, b], slot, rsem.at[index]).start()
                else:
                    device = dev(xh, z, b, xl, yp(away[i]))
                    send(pout.at[i, b], slot, index, device, inside=mine, like=pout_like)

    def result():
        for j in range(2):
            for source in range(4):
                wait_recv(precv.at[j, source], RECV["p"] + j * 4 + source)

            @pl.loop(0, TOK // 32)
            def _(i):
                at = pl.ds(pl.multiple_of(i * 32, 32), 32)
                value = precv[j, 0, at, :].astype(F32)
                for source in range(1, 4):
                    value = value + precv[j, source, at, :].astype(F32)
                kvbuf[j, at, :] = (value * invb[at, :]).astype(BF16)

    for q in range(4):
        task(PLAN["other"][q], g_decode_other, q)
        task(PLAN["own"][q], g_decode_own, q)
        base = PLAN["pair"][q]
        task(base, g_pair, q)
        for step in (2, 3, 4):
            task(base + PLAN["hop"] * (step - 1), g_ring, q, step)
        task(base + PLAN["hop"] * 4, g_final, q)
        task(base + PLAN["hop"] * 4 + PLAN["cross"], g_update, q)
    for n, k in enumerate(H_ORDER):
        start = PLAN["start"][n]
        if k in Y_FIRST:
            for function, after in zip((hy_start, hy_middle, hy_cross, hy_end), PLAN["y"]):
                task(start + after, function, k)
        else:
            for function, after in zip((hx_start, hx_cross, hx_middle, hx_end, hx_last), PLAN["x"]):
                task(start + after, function, k)
    hidden_time = max(item[0] for item in tasks if item[2] in (hy_end, hx_last))
    task(hidden_time + 0.01, ss_send)
    task(hidden_time + 0.02, hidden_ready)
    task(hidden_time + PLAN["squares"], ss_receive)
    for core in range(2):
        for i in range(4):
            base = PLAN["gather"][core] + PLAN["piece"] * i
            for step in range(5):
                task(base + PLAN["relay"] * step, w_step, i, core, step)
            task(max(base + PLAN["relay"] * 4, hidden_time) + 0.1, project, i, core)
    for stage, time in zip((1, 2, 3, 4), PLAN["greet"]):
        task(time, greet, stage)
    task(1000.0, result)
    outs = []
    for _, _, function, arguments in sorted(tasks, key=lambda item: item[:2]):
        function(*arguments)
        if function is g_update and arguments == (3,):
            outs.append(load(newp, params_out, LOCAL["out"]))
            outs.append(load(newm, momentum_out, LOCAL["out"] + 1))
    outs.append(load(kvbuf, kv_out, LOCAL["out"] + 2))
    for index in range(len(sends)):
        wait_send(index)
    for copy in outs:
        copy.wait()


def hand_over(*refs):
    ins, outs, held, sems = refs[:3], refs[3:6], refs[6:9], refs[9]
    loads = [pltpu.make_async_copy(ins[n], held[n], sems.at[n]) for n in range(3)]
    stores = [pltpu.make_async_copy(held[n], outs[n], sems.at[3 + n]) for n in range(3)]
    for copy in loads:
        copy.start()
    for load, store in zip(loads, stores):
        load.wait()
        store.start()
    for copy in stores:
        copy.wait()


def per_device(
    delta_codes, scale_exponents, outer_params, outer_momentum, tensor_partials, residual_stream, norm_gain
):
    ny, nx = len(Y_FIRST), len(X_FIRST)
    vmem = pltpu.VMEM
    scratch = [
        vmem((4, 32, 64, 128), jnp.int32),
        vmem((2, 32, 8, 128), jnp.int32),
        vmem((2, 256, 128), F32),
        vmem((2, 256, 128), F32),
        vmem((TOK, 1024), BF16),
        vmem((64, 128), F32),
        vmem((4, 2, 2, 8, 128, 128), BF16),
        vmem((4, 2, 8, 128, 128), BF16),
        vmem((4, 2, 4, 2, 128, 128), BF16),
        vmem((4, 2, 3, 2, 128, 128), BF16),
        vmem((4, 128, 128), F32),
        vmem((4, 128, 128), BF16),
        vmem((4, 128, 128), BF16),
        vmem((4, 128, 128), F32),
        vmem((2, 256, 128), F32),
        vmem((2, 256, 128), F32),
        vmem((4, 128, 128), BF16),
        vmem((16, 128, 512), BF16),
        vmem((8, TOK, 1024), BF16),
        vmem((8, 2, TOK, 128), BF16),
        vmem((ny, 2, TOK, 128), BF16),
        vmem((8, 2, TOK, 128), BF16),
        vmem((ny, 2, TOK, 128), BF16),
        vmem((8, 2, TOK, 128), BF16),
        vmem((8, 2, TOK, 128), BF16),
        vmem((nx, TOK, 512), BF16),
        vmem((nx, TOK, 512), BF16),
        vmem((2, TOK, 2048), BF16),
        vmem((TOK, 128), F32),
        vmem((8, TOK), F32),
        vmem((4, 8, TOK), F32),
        vmem((4, 2, TOK, 128), BF16),
        vmem((2, 4, TOK, 128), BF16),
        vmem((TOK, 128), F32),
        vmem((2, TOK, 128), BF16),
        pltpu.SemaphoreType.DMA((N_SEND,)),
        pltpu.SemaphoreType.DMA((RECV.total,)),
        pltpu.SemaphoreType.DMA((LOCAL.total,)),
        pltpu.SemaphoreType.REGULAR((4,)),
    ]
    any_spec = pl.BlockSpec(memory_space=pl.ANY)
    out_shape = (
        jax.ShapeDtypeStruct((2, TOK, 128), BF16),
        jax.ShapeDtypeStruct((2, 256, 128), F32),
        jax.ShapeDtypeStruct((2, 256, 128), F32),
    )
    outs = pl.pallas_call(
        kernel,
        out_shape=out_shape,
        in_specs=[any_spec] * 7,
        out_specs=(any_spec,) * 3,
        scratch_shapes=scratch,
        compiler_params=pltpu.CompilerParams(
            collective_id=0, has_side_effects=True, vmem_limit_bytes=60 * 2**20
        ),
        cost_estimate=pl.CostEstimate(flops=2 * 768 * 1024 * 1024, bytes_accessed=13 * 2**20, transcendentals=0),
        name="outer_step",
    )(
        delta_codes.reshape(2, 32, 2, 64, 128),
        scale_exponents.reshape(2, 32, 8, 128),
        outer_params,
        outer_momentum,
        tensor_partials.reshape(TOK, D),
        residual_stream,
        norm_gain.reshape(64, 128),
    )
    return pl.pallas_call(
        hand_over,
        out_shape=out_shape,
        in_specs=[any_spec] * 3,
        out_specs=(any_spec,) * 3,
        scratch_shapes=[vmem(out.shape, out.dtype) for out in out_shape] + [pltpu.SemaphoreType.DMA((6,))],
        name="hand_over",
    )(*outs)


def solution(mesh):
    return jax.shard_map(
        per_device,
        mesh=mesh,
        in_specs=(
            P("replica", None, None, "tensor"),
            P("replica", None, None, "tensor"),
            P(None, "replica", "tensor"),
            P(None, "replica", "tensor"),
            P("tensor", "replica", None),
            P("replica", "tensor"),
            P(),
        ),
        out_specs=(
            P(None, "replica", "tensor"),
            P(None, "replica", "tensor"),
            P(None, "replica", "tensor"),
        ),
        check_vma=False,
    )
```

```python
import jax
import jax.numpy as jnp
from jax import lax
from jax.experimental import pallas as pl
from jax.experimental.pallas import tpu as pltpu
from jax.sharding import PartitionSpec as P

D = 8192
TOK = 384
MESH = pl.DeviceIdType.MESH
F32 = jnp.float32
BF16 = jnp.bfloat16

outer_rate = 0.7
outer_beta = 0.9
norm_epsilon = 1e-05

Y_FIRST = (0, 1, 2, 4, 5, 6, 7)
X_FIRST = (3,)
H_ORDER = (0, 3, 1, 2, 4, 5, 6, 7)
HALF = TOK // 2

PLAN = {
    "other": (1.5, 3.7, 6.8, 10.0),
    "own": (3.0, 5.4, 7.5, 10.7),
    "pair": (4.9, 6.3, 9.6, 13.0),
    "hop": 3.0,
    "cross": 4.2,
    "greet": (6.0, 8.0, 10.0, 11.0),
    "gather": (24.7, 29.7),
    "piece": 0.8,
    "relay": 4.0,
    "start": (3.1, 3.2, 6.5, 10.5, 15.2, 19.9, 24.6, 29.3),
    "y": (0.0, 8.0, 16.0, 23.0),
    "x": (0.0, 11.0, 18.0, 24.0, 29.0),
    "squares": 8.0,
}


class Slots:
    def __init__(self):
        self.total = 0
        self.base = {}

    def add(self, name, count):
        self.base[name] = self.total
        self.total += count

    def __getitem__(self, name):
        return self.base[name]


RECV = Slots()
for _name, _count in (
    ("sib", 4), ("z", 4 * 2 * 4), ("xh", 4), ("a2a", 8), ("ag", 4 * 2 * 4), ("ya", 8 * 2), ("yb", 8 * 2),
    ("yc", 8 * 2), ("xl", 8 * 2), ("asib", 8), ("ss", 4), ("p", 16),
):
    RECV.add(_name, _count)
N_SEND = 256
LOCAL = Slots()
for _name, _count in (("codes", 4), ("part", 8), ("misc", 5), ("out", 9)):
    LOCAL.add(_name, _count)


def decode_nibble(code):
    magnitude = jnp.bitwise_and(code, 7).astype(F32)
    value = jnp.maximum(jnp.maximum(0.5 * magnitude, magnitude - 2.0), 2.0 * magnitude - 8.0)
    return jnp.where(code >= 8, -value, value)


def kernel(
    codes, exps, params, momentum, partials, residual, gain,
    kv_out, params_out, momentum_out,
    cbuf, ebuf, pbuf, mbuf, rbuf, gbuf,
    dec, sibr, zrecv, zout, fin, xout, xrecv, grad, newp, newm, frag, wbuf,
    part, yra, yrb, yrc, yout, xo, xr, xr4, xs, abuf, ssacc, ssout, ssr, pout, precv, invb, kvbuf,
    ssem, rsem, lsem, plane,
):
    r = lax.axis_index("replica")
    t = lax.axis_index("tensor")
    xh = r // 16
    z = lax.rem(r // 2, 8)
    c = lax.rem(r, 2)
    xl = t // 4
    y = lax.rem(t, 4)

    def dev(xh_, z_, c_, xl_, y_):
        return (xh_ * 16 + z_ * 2 + c_, xl_ * 4 + y_)

    def zp(n):
        return lax.rem(z + 8 + n, 8)

    def yp(n):
        return lax.rem(y + 4 + n, 4)

    sibling = dev(xh, z, 1 - c, xl, y)
    x_pair = dev(xh, z, c, 1 - xl, y)
    x_cross = dev(1 - xh, z, c, 1 - xl, y)
    xh_pair = dev(1 - xh, z, c, xl, y)
    z_next = (dev(xh, zp(1), c, xl, y), dev(xh, zp(-1), c, xl, y))
    y_next = (dev(xh, z, c, xl, yp(1)), dev(xh, z, c, xl, yp(-1)))

    sends = []

    def send(src, dst, recv_index, device, cond=None, inside=None, like=None):
        index = len(sends)
        copy = pltpu.make_async_remote_copy(
            src_ref=src, dst_ref=dst, send_sem=ssem.at[index], recv_sem=rsem.at[recv_index],
            device_id=device, device_id_type=MESH,
        )
        if cond is None:
            copy.start()
        else:
            pl.when(cond)(copy.start)
        sends.append((src if like is None else like, cond if inside is None else inside))

    def wait_send(index):
        like, cond = sends[index]
        copy = pltpu.make_async_remote_copy(
            src_ref=like, dst_ref=like, send_sem=ssem.at[index], recv_sem=rsem.at[0],
            device_id=sibling, device_id_type=MESH,
        )
        if cond is None:
            copy.wait_send()
        else:
            pl.when(cond)(copy.wait_send)

    def wait_recv(dst, recv_index):
        pltpu.make_async_remote_copy(
            src_ref=dst, dst_ref=dst, send_sem=ssem.at[0], recv_sem=rsem.at[recv_index],
            device_id=sibling, device_id_type=MESH,
        ).wait_recv()

    def load(src, dst, index):
        copy = pltpu.make_async_copy(src, dst, lsem.at[index])
        copy.start()
        return copy

    code_loads = [None] * 4
    part_loads = [None] * 8

    def load_codes(q):
        code_loads[q] = load(codes.at[q // 2, :, q % 2], cbuf.at[q], LOCAL["codes"] + q)

    def load_part(k):
        part_loads[k] = load(partials.at[:, pl.ds(1024 * k, 1024)], part.at[k], LOCAL["part"] + k)

    load_codes(0)
    exp_load = load(exps, ebuf, LOCAL["misc"])
    res_load = load(residual, rbuf, LOCAL["misc"] + 1)
    first = [2 * (H_ORDER[0] % 4), 2 * (H_ORDER[0] % 4) + 1]
    for k in first:
        load_part(k)
    state_loads = []

    def more_loads():
        load_codes(1)
        rest = [k for u in H_ORDER for k in (2 * (u % 4), 2 * (u % 4) + 1) if u < 4 and k not in first]
        for k in rest[:2]:
            load_part(k)
        load_codes(2)
        load_codes(3)
        for k in rest[2:]:
            load_part(k)
        state_loads.append(load(gain, gbuf, LOCAL["misc"] + 4))
        state_loads.append(load(params, pbuf, LOCAL["misc"] + 2))
        state_loads.append(load(momentum, mbuf, LOCAL["misc"] + 3))

    barrier = pltpu.get_barrier_semaphore()
    for other in (sibling, x_pair, x_cross) + y_next + z_next:
        pl.semaphore_signal(barrier, inc=1, device_id=other, device_id_type=MESH)

    def greet(stage):
        others = (y_next, (x_pair, x_cross), (x_pair, x_cross), (sibling,))
        if stage:
            pl.semaphore_wait(plane.at[stage - 1], len(others[stage - 1]))
        if stage < 4:
            for other in others[stage]:
                pl.semaphore_signal(plane.at[stage], inc=1, device_id=other, device_id_type=MESH)

    def decode(q, core):
        j, half = q // 2, q % 2

        @pl.loop(0, 16)
        def _(i):
            owner = i * 2 + core
            for b in range(4):
                exponent = ebuf[j, owner, pl.ds(4 * half + b, 1), :]
                scale = jnp.left_shift(jnp.ones_like(exponent), exponent + 5).astype(F32) * 2.0**-5
                words = cbuf[q, owner, pl.ds(16 * b, 16), :]
                low = decode_nibble(jnp.bitwise_and(words, 15)) * scale
                high = decode_nibble(jnp.bitwise_and(jnp.right_shift(words, 4), 15)) * scale
                dec[q, core, i // 8, lax.rem(i, 8), pl.ds(16 * b, 16), :] = low.astype(BF16)
                dec[q, core, i // 8, lax.rem(i, 8), pl.ds(64 + 16 * b, 16), :] = high.astype(BF16)

    tasks = []

    def task(time, function, *arguments):
        tasks.append((time, len(tasks), function, arguments))

    def g_decode_other(q):
        code_loads[q].wait()
        if q == 0:
            exp_load.wait()
        decode(q, 1 - c)
        if q == 0:
            pl.semaphore_wait(barrier, 7)
            greet(0)
            more_loads()
        send(dec.at[q, 1 - c], sibr.at[q], RECV["sib"] + q, sibling)

    def g_decode_own(q):
        decode(q, c)

    def g_pair(q):
        wait_recv(sibr.at[q], RECV["sib"] + q)

        @pl.loop(0, 16)
        def _(i):
            a, b = i // 8, lax.rem(i, 8)
            dec[q, c, a, b] = (dec[q, c, a, b].astype(F32) + sibr[q, a, b].astype(F32)).astype(BF16)

        for d in range(2):
            send(dec.at[q, c, d, zp(4)], zrecv.at[q, d, 0, d], RECV["z"] + (q * 2 + d) * 4, z_next[d])

    def g_ring(q, step):
        for d in range(2):
            sign = 1 - 2 * d
            target = zp(sign * (5 - step))
            index = RECV["z"] + (q * 2 + d) * 4 + step - 2
            if step == 2:
                wait_recv(zrecv.at[q, d, 0, d], index)
                zout[q, d, step - 2, d] = (
                    dec[q, c, d, target].astype(F32) + zrecv[q, d, 0, d].astype(F32)
                ).astype(BF16)
                zout[q, d, step - 2, 1 - d] = dec[q, c, 1 - d, target]
            else:
                wait_recv(zrecv.at[q, d, step - 2], index)
                for a in range(2):
                    zout[q, d, step - 2, a] = (
                        dec[q, c, a, target].astype(F32) + zrecv[q, d, step - 2, a].astype(F32)
                    ).astype(BF16)
            send(zout.at[q, d, step - 2], zrecv.at[q, d, step - 1], index + 1, z_next[d])

    def g_final(q):
        for d in range(2):
            wait_recv(zrecv.at[q, d, 3], RECV["z"] + (q * 2 + d) * 4 + 3)

        def total(a):
            return (
                dec[q, c, a, z].astype(F32) + zrecv[q, 0, 3, a].astype(F32) + zrecv[q, 1, 3, a].astype(F32)
            )

        xout[q] = total(1 - xh).astype(BF16)
        send(xout.at[q], xrecv.at[q], RECV["xh"] + q, xh_pair)
        fin[q] = total(xh)

    away = (2, 1, 3, 0)

    def place_of(delta):
        return jnp.where(delta == 2, 0, jnp.where(delta == 1, 1, jnp.where(delta == 3, 2, 3)))

    def g_update(q):
        j, half = q // 2, q % 2
        if q == 0:
            state_loads[1].wait()
            state_loads[2].wait()
        wait_recv(xrecv.at[q], RECV["xh"] + q)
        summed = fin[q] + xrecv[q].astype(F32)
        grad[q, pl.ds(0, 64, stride=2), :] = summed[:64]
        grad[q, pl.ds(1, 64, stride=2), :] = summed[64:]
        outer_grad = grad[q] * (1.0 / 32.0)
        rows = pl.ds(128 * half, 128)
        new_momentum = outer_beta * mbuf[j, rows, :] + outer_grad
        new_params = pbuf[j, rows, :] - outer_rate * (outer_grad + outer_beta * new_momentum)
        newm[j, rows, :] = new_momentum
        newp[j, rows, :] = new_params
        frag[q] = new_params.astype(BF16)
        y_to = 2 * c + half
        column = place_of(lax.rem(y - y_to + 4, 4))
        slot = wbuf.at[xh, z, :, pl.ds(pl.multiple_of(128 * column, 128), 128)]
        index = RECV["a2a"] + xh * 4 + column
        here = (c == j) & (y == y_to)

        @pl.when(here)
        def _():
            pltpu.make_async_copy(frag.at[q], slot, rsem.at[index]).start()

        send(frag.at[q], slot, index, dev(xh, z, j, xl, y_to), jnp.logical_not(here))
        send(frag.at[q], slot, index, dev(1 - xh, z, j, xl, y_to))

    def w_block(source_z, i):
        return wbuf.at[:, source_z, :, pl.ds(128 * i, 128)]

    def w_half(source_z, a, i):
        return wbuf.at[a, source_z, :, pl.ds(128 * i, 128)]

    def w_step(i, core, step):
        like = w_block(0, i) if step < 3 else w_half(0, 0, i)
        mine = c == core

        @pl.when(mine)
        def _():
            if step == 0:
                for a in range(2):
                    wait_recv(w_half(z, a, i), RECV["a2a"] + a * 4 + i)
            for d in range(2):
                index = RECV["ag"] + (i * 2 + d) * 4 + step
                origin = zp((2 * d - 1) * step)
                if 0 < step < 4:
                    wait_recv(w_block(origin, i), index - 1)
                if step < 3:
                    send(w_block(origin, i), w_block(origin, i), index, z_next[d], inside=mine, like=like)
                elif step == 3:
                    piece = w_half(origin, d, i)
                    send(piece, piece, index, z_next[d], inside=mine, like=like)
                else:
                    wait_recv(w_half(origin, d, i), index - 1)

    def lanes(x_, y_):
        return pl.ds(pl.multiple_of(128 * (x_ * 4 + y_), 128), 128)

    def add_rows(out, *terms):
        for g in range(2):
            @pl.loop(0, HALF // 64)
            def _(i):
                at = pl.multiple_of(i * 64, 64)
                value = terms[0](g, at).astype(F32)
                for term in terms[1:]:
                    value = value + term(g, at).astype(F32)
                out(g, at, value)

    def rows(at):
        return pl.ds(at, 64)

    def tokens(u):
        return pl.ds(HALF * (u // 4), HALF)

    def groups(u):
        return pl.ds(2 * (u % 4), 2)

    def part_term(u, own):
        return lambda g, at: part[2 * (u % 4) + g, pl.ds(HALF * (u // 4) + at, 64), own]

    loaded = []

    def h_load(u):
        if u % 4 in loaded:
            return
        loaded.append(u % 4)
        for k in (2 * (u % 4), 2 * (u % 4) + 1):
            part_loads[k].wait()
            if len(loaded) == 1 and k % 2 == 0:
                res_load.wait()

            @pl.when(t == k)
            def _():
                @pl.loop(0, TOK // 16)
                def _(i):
                    at = pl.ds(pl.multiple_of(i * 16, 16), 16)
                    part[k, at, :] = (part[k, at, :].astype(F32) + rbuf[at, :].astype(F32)).astype(BF16)

    def hy_start(u):
        h_load(u)
        for d in range(2):
            send(part.at[groups(u), tokens(u), lanes(d, yp(2))], yra.at[u, d], RECV["ya"] + u * 2 + d, y_next[d])
        for d in range(2):
            piece = part.at[groups(u), tokens(u), lanes(1 - d, yp(1 - 2 * d))]
            send(piece, yrb.at[u, d], RECV["yb"] + u * 2 + d, y_next[d])

    def hy_middle(u):
        for d in range(2):
            wait_recv(yra.at[u, d], RECV["ya"] + u * 2 + d)

            def put(g, at, value, d=d):
                yout[u, d, g, rows(at), :] = value.astype(BF16)

            add_rows(put, part_term(u, lanes(d, yp(1 - 2 * d))), lambda g, at, d=d: yra[u, d, g, rows(at), :])
            send(yout.at[u, d], yrc.at[u, d], RECV["yc"] + u * 2 + d, y_next[d])

    def hy_cross(u):
        for d in range(2):
            wait_recv(yrb.at[u, d], RECV["yb"] + u * 2 + d)
            wait_recv(yrc.at[u, d], RECV["yc"] + u * 2 + d)

        for x_ in range(2):
            def put(g, at, value, x_=x_):
                xo[u, x_, g, rows(at), :] = value.astype(BF16)

            add_rows(
                put, part_term(u, lanes(x_, y)), lambda g, at, x_=x_: yrb[u, 1 - x_, g, rows(at), :],
                lambda g, at, x_=x_: yrc[u, x_, g, rows(at), :],
            )
            send(xo.at[u, x_], xr.at[u, x_], RECV["xl"] + u * 2 + x_, x_pair)

    def finish(u, x_, g, at, value):
        k = 2 * (u % 4) + g
        hidden = value.astype(BF16).astype(F32)
        scaled = hidden * gbuf[pl.ds(8 * k + 4 * x_ + y, 1), :]
        to = pl.ds(HALF * (u // 4) + at, 64)
        abuf[c, to, pl.ds(pl.multiple_of(128 * (2 * k + x_), 128), 128)] = scaled.astype(BF16)
        ssacc[to, :] += hidden * hidden

    def unit_share(core, u):
        return abuf.at[core, tokens(u), pl.ds(512 * (u % 4), 512)]

    def finished(u):
        send(unit_share(c, u), unit_share(c, u), RECV["asib"] + u, sibling)

    gain_waited = []

    def gain_ready():
        if not gain_waited:
            state_loads[0].wait()
            ssacc[...] = jnp.zeros_like(ssacc)
            gain_waited.append(True)

    def hy_end(u):
        gain_ready()
        for x_ in range(2):
            wait_recv(xr.at[u, x_], RECV["xl"] + u * 2 + x_)
            add_rows(
                lambda g, at, value, x_=x_: finish(u, x_, g, at, value),
                lambda g, at, x_=x_: xo[u, x_, g, rows(at), :], lambda g, at, x_=x_: xr[u, x_, g, rows(at), :],
            )
        finished(u)

    def hx_start(u):
        h_load(u)
        other = pl.ds(pl.multiple_of(512 * (1 - xl), 512), 512)
        send(part.at[groups(u), tokens(u), other], xr4.at[X_FIRST.index(u)], RECV["xl"] + u * 2, x_pair)

    def hx_lanes(y_):
        return pl.ds(pl.multiple_of(128 * y_, 128), 128)

    def hx_cross(u):
        n = X_FIRST.index(u)
        wait_recv(xr4.at[n], RECV["xl"] + u * 2)
        own = pl.ds(pl.multiple_of(512 * xl, 512), 512)

        def put(g, at, value):
            xs[n, g, rows(at), :] = value.astype(BF16)

        add_rows(put, part_term(u, own), lambda g, at: xr4[n, g, rows(at), :])
        for d in range(2):
            send(xs.at[n, d, :, hx_lanes(yp(2))], yra.at[u, d, 0], RECV["ya"] + u * 2 + d, y_next[d])

    def hx_middle(u):
        n = X_FIRST.index(u)
        for d in range(2):
            wait_recv(yra.at[u, d, 0], RECV["ya"] + u * 2 + d)
            own = hx_lanes(yp(1 - 2 * d))

            @pl.loop(0, HALF // 64)
            def _(i, d=d, own=own):
                at = rows(pl.multiple_of(i * 64, 64))
                xs[n, d, at, own] = (xs[n, d, at, own].astype(F32) + yra[u, d, 0, at, :].astype(F32)).astype(BF16)

            send(xs.at[n, :, :, own], yrc.at[u, d], RECV["yc"] + u * 2 + d, y_next[d])

    def hx_end(u):
        n = X_FIRST.index(u)
        gain_ready()
        for d in range(2):
            wait_recv(yrc.at[u, d], RECV["yc"] + u * 2 + d)
        own = hx_lanes(y)

        def put(g, at, value):
            xo[u, 0, g, rows(at), :] = value.astype(BF16)
            finish(u, xl, g, at, value)

        add_rows(
            put, lambda g, at: xs[n, g, rows(at), own], lambda g, at: yrc[u, 0, g, rows(at), :],
            lambda g, at: yrc[u, 1, g, rows(at), :],
        )
        send(xo.at[u, 0], xr.at[u, 0], RECV["xl"] + u * 2 + 1, x_pair)

    def hx_last(u):
        wait_recv(xr.at[u, 0], RECV["xl"] + u * 2 + 1)
        add_rows(
            lambda g, at, value: finish(u, 1 - xl, g, at, value), lambda g, at: xr[u, 0, g, rows(at), :]
        )
        finished(u)

    def ss_send():
        for b in range(3):
            block = jnp.sum(ssacc[pl.ds(128 * b, 128), :].T, axis=0, keepdims=True)
            ssout[:, pl.ds(128 * b, 128)] = jnp.broadcast_to(block, (8, 128))
        ssr[y] = ssout[...]
        for e in range(1, 4):
            send(ssout, ssr.at[y], RECV["ss"] + y, dev(xh, z, c, xl, yp(e)))

    def ss_receive():
        for e in range(1, 4):
            wait_recv(ssr.at[yp(e)], RECV["ss"] + yp(e))
        total = ssr[0] + ssr[1] + ssr[2] + ssr[3]
        inverse = lax.rsqrt(total * (1.0 / D) + norm_epsilon) * D**-0.5
        for b in range(3):
            block = jnp.broadcast_to(inverse[0:1, 128 * b : 128 * b + 128], (128, 128))
            invb[pl.ds(128 * b, 128), :] = block.T

    def hidden_ready(th):
        for u in range(4 * th, 4 * th + 4):
            wait_recv(unit_share(1 - c, u), RECV["asib"] + u)

    pout_like = pout.at[0, 0, pl.ds(0, HALF)]

    def project(i, core, th):
        mine = c == core
        at = pl.ds(HALF * th, HALF)

        @pl.when(mine)
        def _():
            w = wbuf[:, :, :, pl.ds(128 * i, 128)].reshape(2048, 128)
            a = abuf[:, at, :].reshape(2 * HALF, 2048)
            products = jnp.dot(a, w, preferred_element_type=F32).astype(BF16)
            for b in range(2):
                pout[i, b, at, :] = products[b * HALF : b * HALF + HALF]
            for b in range(2):
                piece = pout.at[i, b, at]
                slot = precv.at[core, y, at]
                index = RECV["p"] + (core * 4 + y) * 2 + th
                if away[i] == 0 and b == core:
                    pltpu.make_async_copy(piece, slot, rsem.at[index]).start()
                else:
                    device = dev(xh, z, b, xl, yp(away[i]))
                    send(piece, slot, index, device, inside=mine, like=pout_like)

    def result(th):
        for j in range(2):
            for source in range(4):
                wait_recv(precv.at[j, source, pl.ds(HALF * th, HALF)], RECV["p"] + (j * 4 + source) * 2 + th)

            @pl.loop(0, HALF // 32)
            def _(i):
                at = pl.ds(pl.multiple_of(HALF * th + i * 32, 32), 32)
                value = precv[j, 0, at, :].astype(F32)
                for source in range(1, 4):
                    value = value + precv[j, source, at, :].astype(F32)
                kvbuf[j, at, :] = (value * invb[at, :]).astype(BF16)

    for q in range(4):
        task(PLAN["other"][q], g_decode_other, q)
        task(PLAN["own"][q], g_decode_own, q)
        base = PLAN["pair"][q]
        task(base, g_pair, q)
        for step in (2, 3, 4):
            task(base + PLAN["hop"] * (step - 1), g_ring, q, step)
        task(base + PLAN["hop"] * 4, g_final, q)
        task(base + PLAN["hop"] * 4 + PLAN["cross"], g_update, q)
        task(PLAN["greet"][q], greet, q + 1)
    ready = [0.0, 0.0]
    for n, u in enumerate(H_ORDER):
        start = PLAN["start"][n]
        if u in Y_FIRST:
            steps = zip((hy_start, hy_middle, hy_cross, hy_end), PLAN["y"])
        else:
            steps = zip((hx_start, hx_cross, hx_middle, hx_end, hx_last), PLAN["x"])
        for function, after in steps:
            task(start + after, function, u)
            ready[u // 4] = max(ready[u // 4], start + after)
    ready[1] = max(ready) + 0.01
    for th in range(2):
        task(ready[th] + 0.5, hidden_ready, th)
    task(ready[1] + 0.3, ss_send)
    for core in range(2):
        for i in range(4):
            base = PLAN["gather"][core] + PLAN["piece"] * i
            for step in range(5):
                task(base + PLAN["relay"] * step, w_step, i, core, step)
            for th in range(2):
                task(max(base + PLAN["relay"] * 4, ready[th] + 0.5) + 0.1, project, i, core, th)
    end = max(item[0] for item in tasks)
    task(ready[1] + PLAN["squares"], ss_receive)
    task(max(end, ready[1] + PLAN["squares"]) + 1.0, result, 0)
    task(max(end, ready[1] + PLAN["squares"]) + 2.0, result, 1)
    outs = []
    for _, _, function, arguments in sorted(tasks, key=lambda item: item[:2]):
        function(*arguments)
        if function is g_update and arguments == (3,):
            outs.append(load(newp, params_out, LOCAL["out"]))
            outs.append(load(newm, momentum_out, LOCAL["out"] + 1))
    outs.append(load(kvbuf, kv_out, LOCAL["out"] + 2))
    for index in range(len(sends)):
        wait_send(index)
    for copy in outs:
        copy.wait()


def hand_over(*refs):
    ins, outs, held, sems = refs[:3], refs[3:6], refs[6:9], refs[9]
    loads = [pltpu.make_async_copy(ins[n], held[n], sems.at[n]) for n in range(3)]
    stores = [pltpu.make_async_copy(held[n], outs[n], sems.at[3 + n]) for n in range(3)]
    for copy in loads:
        copy.start()
    for load, store in zip(loads, stores):
        load.wait()
        store.start()
    for copy in stores:
        copy.wait()


def per_device(
    delta_codes, scale_exponents, outer_params, outer_momentum, tensor_partials, residual_stream, norm_gain
):
    nx = max(len(X_FIRST), 1)
    vmem = pltpu.VMEM
    scratch = [
        vmem((4, 32, 64, 128), jnp.int32),
        vmem((2, 32, 8, 128), jnp.int32),
        vmem((2, 256, 128), F32),
        vmem((2, 256, 128), F32),
        vmem((TOK, 1024), BF16),
        vmem((64, 128), F32),
        vmem((4, 2, 2, 8, 128, 128), BF16),
        vmem((4, 2, 8, 128, 128), BF16),
        vmem((4, 2, 4, 2, 128, 128), BF16),
        vmem((4, 2, 3, 2, 128, 128), BF16),
        vmem((4, 128, 128), F32),
        vmem((4, 128, 128), BF16),
        vmem((4, 128, 128), BF16),
        vmem((4, 128, 128), F32),
        vmem((2, 256, 128), F32),
        vmem((2, 256, 128), F32),
        vmem((4, 128, 128), BF16),
        vmem((2, 8, 128, 512), BF16),
        vmem((8, TOK, 1024), BF16),
        vmem((8, 2, 2, HALF, 128), BF16),
        vmem((8, 2, 2, HALF, 128), BF16),
        vmem((8, 2, 2, HALF, 128), BF16),
        vmem((8, 2, 2, HALF, 128), BF16),
        vmem((8, 2, 2, HALF, 128), BF16),
        vmem((8, 2, 2, HALF, 128), BF16),
        vmem((nx, 2, HALF, 512), BF16),
        vmem((nx, 2, HALF, 512), BF16),
        vmem((2, TOK, 2048), BF16),
        vmem((TOK, 128), F32),
        vmem((8, TOK), F32),
        vmem((4, 8, TOK), F32),
        vmem((4, 2, TOK, 128), BF16),
        vmem((2, 4, TOK, 128), BF16),
        vmem((TOK, 128), F32),
        vmem((2, TOK, 128), BF16),
        pltpu.SemaphoreType.DMA((N_SEND,)),
        pltpu.SemaphoreType.DMA((RECV.total,)),
        pltpu.SemaphoreType.DMA((LOCAL.total,)),
        pltpu.SemaphoreType.REGULAR((4,)),
    ]
    any_spec = pl.BlockSpec(memory_space=pl.ANY)
    out_shape = (
        jax.ShapeDtypeStruct((2, TOK, 128), BF16),
        jax.ShapeDtypeStruct((2, 256, 128), F32),
        jax.ShapeDtypeStruct((2, 256, 128), F32),
    )
    outs = pl.pallas_call(
        kernel,
        out_shape=out_shape,
        in_specs=[any_spec] * 7,
        out_specs=(any_spec,) * 3,
        scratch_shapes=scratch,
        compiler_params=pltpu.CompilerParams(
            collective_id=0, has_side_effects=True, vmem_limit_bytes=60 * 2**20
        ),
        cost_estimate=pl.CostEstimate(flops=2 * 768 * 1024 * 1024, bytes_accessed=13 * 2**20, transcendentals=0),
        name="outer_step",
    )(
        delta_codes.reshape(2, 32, 2, 64, 128),
        scale_exponents.reshape(2, 32, 8, 128),
        outer_params,
        outer_momentum,
        tensor_partials.reshape(TOK, D),
        residual_stream,
        norm_gain.reshape(64, 128),
    )
    return pl.pallas_call(
        hand_over,
        out_shape=out_shape,
        in_specs=[any_spec] * 3,
        out_specs=(any_spec,) * 3,
        scratch_shapes=[vmem(out.shape, out.dtype) for out in out_shape] + [pltpu.SemaphoreType.DMA((6,))],
        name="hand_over",
    )(*outs)


def solution(mesh):
    return jax.shard_map(
        per_device,
        mesh=mesh,
        in_specs=(
            P("replica", None, None, "tensor"),
            P("replica", None, None, "tensor"),
            P(None, "replica", "tensor"),
            P(None, "replica", "tensor"),
            P("tensor", "replica", None),
            P("replica", "tensor"),
            P(),
        ),
        out_specs=(
            P(None, "replica", "tensor"),
            P(None, "replica", "tensor"),
            P(None, "replica", "tensor"),
        ),
        check_vma=False,
    )
```

```python
import jax
import jax.numpy as jnp
from jax import lax
from jax.experimental import pallas as pl
from jax.experimental.pallas import tpu as pltpu
from jax.sharding import PartitionSpec as P

D = 8192
TOK = 384
MESH = pl.DeviceIdType.MESH
F32 = jnp.float32
BF16 = jnp.bfloat16

outer_rate = 0.7
outer_beta = 0.9
norm_epsilon = 1e-05

Y_FIRST = (0, 1, 2, 4, 5, 6, 7)
X_FIRST = (3,)
H_ORDER = (0, 3, 1, 2, 4, 5, 6, 7)
HALF = TOK // 2

PLAN = {
    "other": (1.5, 3.7, 6.8, 10.0),
    "own": (3.0, 5.4, 7.5, 10.7),
    "pair": (4.9, 6.3, 9.6, 13.0),
    "hop": 3.0,
    "cross": 4.2,
    "greet": (6.0, 8.0, 10.0, 11.0),
    "gather": (23.2, 29.7),
    "piece": 0.9,
    "relay": 4.0,
    "start": (3.1, 3.2, 6.5, 10.5, 15.2, 19.9, 24.6, 29.3),
    "y": (0.0, 8.0, 16.0, 23.0),
    "x": (0.0, 11.0, 18.0, 24.0, 29.0),
    "squares": 8.0,
}


class Slots:
    def __init__(self):
        self.total = 0
        self.base = {}

    def add(self, name, count):
        self.base[name] = self.total
        self.total += count

    def __getitem__(self, name):
        return self.base[name]


RECV = Slots()
for _name, _count in (
    ("sib", 4), ("z", 4 * 2 * 4), ("xh", 4), ("a2a", 8), ("ag", 4 * 2 * 4), ("ya", 8 * 2), ("yb", 8 * 2),
    ("yc", 8 * 2), ("xl", 8 * 2), ("asib", 8), ("ss", 4), ("p", 16),
):
    RECV.add(_name, _count)
N_SEND = 256
LOCAL = Slots()
for _name, _count in (("codes", 4), ("part", 8), ("misc", 5), ("out", 9)):
    LOCAL.add(_name, _count)


def decode_nibble(code):
    magnitude = jnp.bitwise_and(code, 7).astype(F32)
    value = jnp.maximum(jnp.maximum(0.5 * magnitude, magnitude - 2.0), 2.0 * magnitude - 8.0)
    return jnp.where(code >= 8, -value, value)


def kernel(
    codes, exps, params, momentum, partials, residual, gain,
    kv_out, params_out, momentum_out,
    cbuf, ebuf, pbuf, mbuf, rbuf, gbuf,
    dec, sibr, zrecv, zout, fin, xout, xrecv, grad, newp, newm, frag, wbuf,
    part, yra, yrb, yrc, yout, xo, xr, xr4, xs, abuf, ssacc, ssout, ssr, pout, precv, invb, kvbuf,
    ssem, rsem, lsem, plane,
):
    r = lax.axis_index("replica")
    t = lax.axis_index("tensor")
    xh = r // 16
    z = lax.rem(r // 2, 8)
    c = lax.rem(r, 2)
    xl = t // 4
    y = lax.rem(t, 4)

    def dev(xh_, z_, c_, xl_, y_):
        return (xh_ * 16 + z_ * 2 + c_, xl_ * 4 + y_)

    def zp(n):
        return lax.rem(z + 8 + n, 8)

    def yp(n):
        return lax.rem(y + 4 + n, 4)

    sibling = dev(xh, z, 1 - c, xl, y)
    x_pair = dev(xh, z, c, 1 - xl, y)
    x_cross = dev(1 - xh, z, c, 1 - xl, y)
    xh_pair = dev(1 - xh, z, c, xl, y)
    z_next = (dev(xh, zp(1), c, xl, y), dev(xh, zp(-1), c, xl, y))
    y_next = (dev(xh, z, c, xl, yp(1)), dev(xh, z, c, xl, yp(-1)))

    sends = []

    def send(src, dst, recv_index, device, cond=None, inside=None, like=None):
        index = len(sends)
        copy = pltpu.make_async_remote_copy(
            src_ref=src, dst_ref=dst, send_sem=ssem.at[index], recv_sem=rsem.at[recv_index],
            device_id=device, device_id_type=MESH,
        )
        if cond is None:
            copy.start()
        else:
            pl.when(cond)(copy.start)
        sends.append((src if like is None else like, cond if inside is None else inside))

    def wait_send(index):
        like, cond = sends[index]
        copy = pltpu.make_async_remote_copy(
            src_ref=like, dst_ref=like, send_sem=ssem.at[index], recv_sem=rsem.at[0],
            device_id=sibling, device_id_type=MESH,
        )
        if cond is None:
            copy.wait_send()
        else:
            pl.when(cond)(copy.wait_send)

    def wait_recv(dst, recv_index):
        pltpu.make_async_remote_copy(
            src_ref=dst, dst_ref=dst, send_sem=ssem.at[0], recv_sem=rsem.at[recv_index],
            device_id=sibling, device_id_type=MESH,
        ).wait_recv()

    def load(src, dst, index):
        copy = pltpu.make_async_copy(src, dst, lsem.at[index])
        copy.start()
        return copy

    code_loads = [None] * 4
    part_loads = [None] * 8

    def load_codes(q):
        code_loads[q] = load(codes.at[q // 2, :, q % 2], cbuf.at[q], LOCAL["codes"] + q)

    def load_part(k):
        part_loads[k] = load(partials.at[:, pl.ds(1024 * k, 1024)], part.at[k], LOCAL["part"] + k)

    load_codes(0)
    exp_load = load(exps, ebuf, LOCAL["misc"])
    res_load = load(residual, rbuf, LOCAL["misc"] + 1)
    first = [2 * (H_ORDER[0] % 4), 2 * (H_ORDER[0] % 4) + 1]
    for k in first:
        load_part(k)
    state_loads = []

    def more_loads():
        load_codes(1)
        rest = [k for u in H_ORDER for k in (2 * (u % 4), 2 * (u % 4) + 1) if u < 4 and k not in first]
        for k in rest[:2]:
            load_part(k)
        load_codes(2)
        load_codes(3)
        for k in rest[2:]:
            load_part(k)
        state_loads.append(load(gain, gbuf, LOCAL["misc"] + 4))
        state_loads.append(load(params, pbuf, LOCAL["misc"] + 2))
        state_loads.append(load(momentum, mbuf, LOCAL["misc"] + 3))

    barrier = pltpu.get_barrier_semaphore()
    for other in (sibling, x_pair, x_cross) + y_next + z_next:
        pl.semaphore_signal(barrier, inc=1, device_id=other, device_id_type=MESH)

    def greet(stage):
        others = (y_next, (x_pair, x_cross), (x_pair, x_cross), (sibling,))
        if stage:
            pl.semaphore_wait(plane.at[stage - 1], len(others[stage - 1]))
        if stage < 4:
            for other in others[stage]:
                pl.semaphore_signal(plane.at[stage], inc=1, device_id=other, device_id_type=MESH)

    def decode(q, core):
        j, half = q // 2, q % 2

        @pl.loop(0, 16)
        def _(i):
            owner = i * 2 + core
            for b in range(4):
                exponent = ebuf[j, owner, pl.ds(4 * half + b, 1), :]
                scale = jnp.left_shift(jnp.ones_like(exponent), exponent + 5).astype(F32) * 2.0**-5
                words = cbuf[q, owner, pl.ds(16 * b, 16), :]
                low = decode_nibble(jnp.bitwise_and(words, 15)) * scale
                high = decode_nibble(jnp.bitwise_and(jnp.right_shift(words, 4), 15)) * scale
                dec[q, core, i // 8, lax.rem(i, 8), pl.ds(16 * b, 16), :] = low.astype(BF16)
                dec[q, core, i // 8, lax.rem(i, 8), pl.ds(64 + 16 * b, 16), :] = high.astype(BF16)

    tasks = []

    def task(time, function, *arguments):
        tasks.append((time, len(tasks), function, arguments))

    def g_decode_other(q):
        code_loads[q].wait()
        if q == 0:
            exp_load.wait()
        decode(q, 1 - c)
        if q == 0:
            pl.semaphore_wait(barrier, 7)
            greet(0)
            more_loads()
        send(dec.at[q, 1 - c], sibr.at[q], RECV["sib"] + q, sibling)

    def g_decode_own(q):
        decode(q, c)

    def g_pair(q):
        wait_recv(sibr.at[q], RECV["sib"] + q)

        @pl.loop(0, 16)
        def _(i):
            a, b = i // 8, lax.rem(i, 8)
            dec[q, c, a, b] = (dec[q, c, a, b].astype(F32) + sibr[q, a, b].astype(F32)).astype(BF16)

        for d in range(2):
            send(dec.at[q, c, d, zp(4)], zrecv.at[q, d, 0, d], RECV["z"] + (q * 2 + d) * 4, z_next[d])

    def g_ring(q, step):
        for d in range(2):
            sign = 1 - 2 * d
            target = zp(sign * (5 - step))
            index = RECV["z"] + (q * 2 + d) * 4 + step - 2
            if step == 2:
                wait_recv(zrecv.at[q, d, 0, d], index)
                zout[q, d, step - 2, d] = (
                    dec[q, c, d, target].astype(F32) + zrecv[q, d, 0, d].astype(F32)
                ).astype(BF16)
                zout[q, d, step - 2, 1 - d] = dec[q, c, 1 - d, target]
            else:
                wait_recv(zrecv.at[q, d, step - 2], index)
                for a in range(2):
                    zout[q, d, step - 2, a] = (
                        dec[q, c, a, target].astype(F32) + zrecv[q, d, step - 2, a].astype(F32)
                    ).astype(BF16)
            send(zout.at[q, d, step - 2], zrecv.at[q, d, step - 1], index + 1, z_next[d])

    def g_final(q):
        for d in range(2):
            wait_recv(zrecv.at[q, d, 3], RECV["z"] + (q * 2 + d) * 4 + 3)

        def total(a):
            return (
                dec[q, c, a, z].astype(F32) + zrecv[q, 0, 3, a].astype(F32) + zrecv[q, 1, 3, a].astype(F32)
            )

        xout[q] = total(1 - xh).astype(BF16)
        send(xout.at[q], xrecv.at[q], RECV["xh"] + q, xh_pair)
        fin[q] = total(xh)

    away = (2, 1, 3, 0)

    def place_of(delta):
        return jnp.where(delta == 2, 0, jnp.where(delta == 1, 1, jnp.where(delta == 3, 2, 3)))

    def g_update(q):
        j, half = q // 2, q % 2
        if q == 0:
            state_loads[1].wait()
            state_loads[2].wait()
        wait_recv(xrecv.at[q], RECV["xh"] + q)
        summed = fin[q] + xrecv[q].astype(F32)
        grad[q, pl.ds(0, 64, stride=2), :] = summed[:64]
        grad[q, pl.ds(1, 64, stride=2), :] = summed[64:]
        outer_grad = grad[q] * (1.0 / 32.0)
        rows = pl.ds(128 * half, 128)
        new_momentum = outer_beta * mbuf[j, rows, :] + outer_grad
        new_params = pbuf[j, rows, :] - outer_rate * (outer_grad + outer_beta * new_momentum)
        newm[j, rows, :] = new_momentum
        newp[j, rows, :] = new_params
        frag[q] = new_params.astype(BF16)
        y_to = 2 * c + half
        column = place_of(lax.rem(y - y_to + 4, 4))
        slot = wbuf.at[xh, z, :, pl.ds(pl.multiple_of(128 * column, 128), 128)]
        index = RECV["a2a"] + xh * 4 + column
        here = (c == j) & (y == y_to)

        @pl.when(here)
        def _():
            pltpu.make_async_copy(frag.at[q], slot, rsem.at[index]).start()

        send(frag.at[q], slot, index, dev(xh, z, j, xl, y_to), jnp.logical_not(here))
        send(frag.at[q], slot, index, dev(1 - xh, z, j, xl, y_to))

    def w_block(source_z, i):
        return wbuf.at[:, source_z, :, pl.ds(128 * i, 128)]

    def w_half(source_z, a, i):
        return wbuf.at[a, source_z, :, pl.ds(128 * i, 128)]

    def w_step(i, core, step):
        like = w_block(0, i) if step < 3 else w_half(0, 0, i)
        mine = c == core

        @pl.when(mine)
        def _():
            if step == 0:
                for a in range(2):
                    wait_recv(w_half(z, a, i), RECV["a2a"] + a * 4 + i)
            for d in range(2):
                index = RECV["ag"] + (i * 2 + d) * 4 + step
                origin = zp((2 * d - 1) * step)
                if 0 < step < 4:
                    wait_recv(w_block(origin, i), index - 1)
                if step < 3:
                    send(w_block(origin, i), w_block(origin, i), index, z_next[d], inside=mine, like=like)
                elif step == 3:
                    piece = w_half(origin, d, i)
                    send(piece, piece, index, z_next[d], inside=mine, like=like)
                else:
                    wait_recv(w_half(origin, d, i), index - 1)

    def lanes(x_, y_):
        return pl.ds(pl.multiple_of(128 * (x_ * 4 + y_), 128), 128)

    def add_rows(out, *terms):
        for g in range(2):
            @pl.loop(0, HALF // 64)
            def _(i):
                at = pl.multiple_of(i * 64, 64)
                value = terms[0](g, at).astype(F32)
                for term in terms[1:]:
                    value = value + term(g, at).astype(F32)
                out(g, at, value)

    def rows(at):
        return pl.ds(at, 64)

    def tokens(u):
        return pl.ds(HALF * (u // 4), HALF)

    def groups(u):
        return pl.ds(2 * (u % 4), 2)

    def part_term(u, own):
        return lambda g, at: part[2 * (u % 4) + g, pl.ds(HALF * (u // 4) + at, 64), own]

    loaded = []

    def h_load(u):
        if u % 4 in loaded:
            return
        loaded.append(u % 4)
        for k in (2 * (u % 4), 2 * (u % 4) + 1):
            part_loads[k].wait()
            if len(loaded) == 1 and k % 2 == 0:
                res_load.wait()

            @pl.when(t == k)
            def _():
                @pl.loop(0, TOK // 16)
                def _(i):
                    at = pl.ds(pl.multiple_of(i * 16, 16), 16)
                    part[k, at, :] = (part[k, at, :].astype(F32) + rbuf[at, :].astype(F32)).astype(BF16)

    def hy_start(u):
        h_load(u)
        for d in range(2):
            send(part.at[groups(u), tokens(u), lanes(d, yp(2))], yra.at[u, d], RECV["ya"] + u * 2 + d, y_next[d])
        for d in range(2):
            piece = part.at[groups(u), tokens(u), lanes(1 - d, yp(1 - 2 * d))]
            send(piece, yrb.at[u, d], RECV["yb"] + u * 2 + d, y_next[d])

    def hy_middle(u):
        for d in range(2):
            wait_recv(yra.at[u, d], RECV["ya"] + u * 2 + d)

            def put(g, at, value, d=d):
                yout[u, d, g, rows(at), :] = value.astype(BF16)

            add_rows(put, part_term(u, lanes(d, yp(1 - 2 * d))), lambda g, at, d=d: yra[u, d, g, rows(at), :])
            send(yout.at[u, d], yrc.at[u, d], RECV["yc"] + u * 2 + d, y_next[d])

    def hy_cross(u):
        for d in range(2):
            wait_recv(yrb.at[u, d], RECV["yb"] + u * 2 + d)
            wait_recv(yrc.at[u, d], RECV["yc"] + u * 2 + d)

        for x_ in range(2):
            def put(g, at, value, x_=x_):
                xo[u, x_, g, rows(at), :] = value.astype(BF16)

            add_rows(
                put, part_term(u, lanes(x_, y)), lambda g, at, x_=x_: yrb[u, 1 - x_, g, rows(at), :],
                lambda g, at, x_=x_: yrc[u, x_, g, rows(at), :],
            )
            send(xo.at[u, x_], xr.at[u, x_], RECV["xl"] + u * 2 + x_, x_pair)

    def finish(u, x_, g, at, value):
        k = 2 * (u % 4) + g
        hidden = value.astype(BF16).astype(F32)
        scaled = hidden * gbuf[pl.ds(8 * k + 4 * x_ + y, 1), :]
        to = pl.ds(HALF * (u // 4) + at, 64)
        abuf[c, to, pl.ds(pl.multiple_of(128 * (2 * k + x_), 128), 128)] = scaled.astype(BF16)
        ssacc[to, :] += hidden * hidden

    def unit_share(core, u):
        return abuf.at[core, tokens(u), pl.ds(512 * (u % 4), 512)]

    def finished(u):
        send(unit_share(c, u), unit_share(c, u), RECV["asib"] + u, sibling)

    gain_waited = []

    def gain_ready():
        if not gain_waited:
            state_loads[0].wait()
            ssacc[...] = jnp.zeros_like(ssacc)
            gain_waited.append(True)

    def hy_end(u):
        gain_ready()
        for x_ in range(2):
            wait_recv(xr.at[u, x_], RECV["xl"] + u * 2 + x_)
            add_rows(
                lambda g, at, value, x_=x_: finish(u, x_, g, at, value),
                lambda g, at, x_=x_: xo[u, x_, g, rows(at), :], lambda g, at, x_=x_: xr[u, x_, g, rows(at), :],
            )
        finished(u)

    def hx_start(u):
        h_load(u)
        other = pl.ds(pl.multiple_of(512 * (1 - xl), 512), 512)
        send(part.at[groups(u), tokens(u), other], xr4.at[X_FIRST.index(u)], RECV["xl"] + u * 2, x_pair)

    def hx_lanes(y_):
        return pl.ds(pl.multiple_of(128 * y_, 128), 128)

    def hx_cross(u):
        n = X_FIRST.index(u)
        wait_recv(xr4.at[n], RECV["xl"] + u * 2)
        own = pl.ds(pl.multiple_of(512 * xl, 512), 512)

        def put(g, at, value):
            xs[n, g, rows(at), :] = value.astype(BF16)

        add_rows(put, part_term(u, own), lambda g, at: xr4[n, g, rows(at), :])
        for d in range(2):
            send(xs.at[n, d, :, hx_lanes(yp(2))], yra.at[u, d, 0], RECV["ya"] + u * 2 + d, y_next[d])

    def hx_middle(u):
        n = X_FIRST.index(u)
        for d in range(2):
            wait_recv(yra.at[u, d, 0], RECV["ya"] + u * 2 + d)
            own = hx_lanes(yp(1 - 2 * d))

            @pl.loop(0, HALF // 64)
            def _(i, d=d, own=own):
                at = rows(pl.multiple_of(i * 64, 64))
                xs[n, d, at, own] = (xs[n, d, at, own].astype(F32) + yra[u, d, 0, at, :].astype(F32)).astype(BF16)

            send(xs.at[n, :, :, own], yrc.at[u, d], RECV["yc"] + u * 2 + d, y_next[d])

    def hx_end(u):
        n = X_FIRST.index(u)
        gain_ready()
        for d in range(2):
            wait_recv(yrc.at[u, d], RECV["yc"] + u * 2 + d)
        own = hx_lanes(y)

        def put(g, at, value):
            xo[u, 0, g, rows(at), :] = value.astype(BF16)
            finish(u, xl, g, at, value)

        add_rows(
            put, lambda g, at: xs[n, g, rows(at), own], lambda g, at: yrc[u, 0, g, rows(at), :],
            lambda g, at: yrc[u, 1, g, rows(at), :],
        )
        send(xo.at[u, 0], xr.at[u, 0], RECV["xl"] + u * 2 + 1, x_pair)

    def hx_last(u):
        wait_recv(xr.at[u, 0], RECV["xl"] + u * 2 + 1)
        add_rows(
            lambda g, at, value: finish(u, 1 - xl, g, at, value), lambda g, at: xr[u, 0, g, rows(at), :]
        )
        finished(u)

    def ss_send():
        for b in range(3):
            block = jnp.sum(ssacc[pl.ds(128 * b, 128), :].T, axis=0, keepdims=True)
            ssout[:, pl.ds(128 * b, 128)] = jnp.broadcast_to(block, (8, 128))
        ssr[y] = ssout[...]
        for e in range(1, 4):
            send(ssout, ssr.at[y], RECV["ss"] + y, dev(xh, z, c, xl, yp(e)))

    def ss_receive():
        for e in range(1, 4):
            wait_recv(ssr.at[yp(e)], RECV["ss"] + yp(e))
        total = ssr[0] + ssr[1] + ssr[2] + ssr[3]
        inverse = lax.rsqrt(total * (1.0 / D) + norm_epsilon) * D**-0.5
        for b in range(3):
            block = jnp.broadcast_to(inverse[0:1, 128 * b : 128 * b + 128], (128, 128))
            invb[pl.ds(128 * b, 128), :] = block.T

    def hidden_ready(th):
        for u in range(4 * th, 4 * th + 4):
            wait_recv(unit_share(1 - c, u), RECV["asib"] + u)

    pout_like = pout.at[0, 0, pl.ds(0, HALF)]

    def project(i, core, th):
        mine = c == core
        at = pl.ds(HALF * th, HALF)

        @pl.when(mine)
        def _():
            w = wbuf[:, :, :, pl.ds(128 * i, 128)].reshape(2048, 128)
            a = abuf[:, at, :].reshape(2 * HALF, 2048)
            products = jnp.dot(a, w, preferred_element_type=F32).astype(BF16)
            for b in range(2):
                pout[i, b, at, :] = products[b * HALF : b * HALF + HALF]
            for b in range(2):
                piece = pout.at[i, b, at]
                slot = precv.at[core, y, at]
                index = RECV["p"] + (core * 4 + y) * 2 + th
                if away[i] == 0 and b == core:
                    pltpu.make_async_copy(piece, slot, rsem.at[index]).start()
                else:
                    device = dev(xh, z, b, xl, yp(away[i]))
                    send(piece, slot, index, device, inside=mine, like=pout_like)

    def result(th):
        for j in range(2):
            for source in range(4):
                wait_recv(precv.at[j, source, pl.ds(HALF * th, HALF)], RECV["p"] + (j * 4 + source) * 2 + th)

            @pl.loop(0, HALF // 32)
            def _(i):
                at = pl.ds(pl.multiple_of(HALF * th + i * 32, 32), 32)
                value = precv[j, 0, at, :].astype(F32)
                for source in range(1, 4):
                    value = value + precv[j, source, at, :].astype(F32)
                kvbuf[j, at, :] = (value * invb[at, :]).astype(BF16)

    for q in range(4):
        task(PLAN["other"][q], g_decode_other, q)
        task(PLAN["own"][q], g_decode_own, q)
        base = PLAN["pair"][q]
        task(base, g_pair, q)
        for step in (2, 3, 4):
            task(base + PLAN["hop"] * (step - 1), g_ring, q, step)
        task(base + PLAN["hop"] * 4, g_final, q)
        task(base + PLAN["hop"] * 4 + PLAN["cross"], g_update, q)
        task(PLAN["greet"][q], greet, q + 1)
    ready = [0.0, 0.0]
    for n, u in enumerate(H_ORDER):
        start = PLAN["start"][n]
        if u in Y_FIRST:
            steps = zip((hy_start, hy_middle, hy_cross, hy_end), PLAN["y"])
        else:
            steps = zip((hx_start, hx_cross, hx_middle, hx_end, hx_last), PLAN["x"])
        for function, after in steps:
            task(start + after, function, u)
            ready[u // 4] = max(ready[u // 4], start + after)
    ready[1] = max(ready) + 0.01
    for th in range(2):
        task(ready[th] + 0.5, hidden_ready, th)
    task(ready[1] + 0.3, ss_send)
    for core in range(2):
        for i in range(4):
            base = PLAN["gather"][core] + PLAN["piece"] * i
            for step in range(5):
                task(base + PLAN["relay"] * step, w_step, i, core, step)
            for th in range(2):
                task(max(base + PLAN["relay"] * 4, ready[th] + 0.5) + 0.1, project, i, core, th)
    end = max(item[0] for item in tasks)
    task(ready[1] + PLAN["squares"], ss_receive)
    task(max(end, ready[1] + PLAN["squares"]) + 1.0, result, 0)
    task(max(end, ready[1] + PLAN["squares"]) + 2.0, result, 1)
    outs = []
    drained = 0

    def drain(limit, most):
        count = max(0, min(most, limit - drained))
        for index in range(drained, drained + count):
            wait_send(index)
        return drained + count

    for _, _, function, arguments in sorted(tasks, key=lambda item: item[:2]):
        if function is result and arguments == (0,):
            drained = drain(len(sends) - 16, len(sends))
        function(*arguments)
        if function is g_update and arguments == (3,):
            outs.append(load(newp, params_out, LOCAL["out"]))
            outs.append(load(newm, momentum_out, LOCAL["out"] + 1))
        if function is result:
            half = pl.ds(HALF * arguments[0], HALF)
            outs.append(load(kvbuf.at[:, half], kv_out.at[:, half], LOCAL["out"] + 2 + arguments[0]))
        else:
            drained = drain(len(sends) - 48, 6)
    drained = drain(len(sends), len(sends))
    for copy in outs:
        copy.wait()


def hand_over(*refs):
    ins, outs, held, sems = refs[:3], refs[3:6], refs[6:9], refs[9]
    loads = [pltpu.make_async_copy(ins[n], held[n], sems.at[n]) for n in range(3)]
    stores = [pltpu.make_async_copy(held[n], outs[n], sems.at[3 + n]) for n in range(3)]
    for copy in loads:
        copy.start()
    for load, store in zip(loads, stores):
        load.wait()
        store.start()
    for copy in stores:
        copy.wait()


def per_device(
    delta_codes, scale_exponents, outer_params, outer_momentum, tensor_partials, residual_stream, norm_gain
):
    nx = max(len(X_FIRST), 1)
    vmem = pltpu.VMEM
    scratch = [
        vmem((4, 32, 64, 128), jnp.int32),
        vmem((2, 32, 8, 128), jnp.int32),
        vmem((2, 256, 128), F32),
        vmem((2, 256, 128), F32),
        vmem((TOK, 1024), BF16),
        vmem((64, 128), F32),
        vmem((4, 2, 2, 8, 128, 128), BF16),
        vmem((4, 2, 8, 128, 128), BF16),
        vmem((4, 2, 4, 2, 128, 128), BF16),
        vmem((4, 2, 3, 2, 128, 128), BF16),
        vmem((4, 128, 128), F32),
        vmem((4, 128, 128), BF16),
        vmem((4, 128, 128), BF16),
        vmem((4, 128, 128), F32),
        vmem((2, 256, 128), F32),
        vmem((2, 256, 128), F32),
        vmem((4, 128, 128), BF16),
        vmem((2, 8, 128, 512), BF16),
        vmem((8, TOK, 1024), BF16),
        vmem((8, 2, 2, HALF, 128), BF16),
        vmem((8, 2, 2, HALF, 128), BF16),
        vmem((8, 2, 2, HALF, 128), BF16),
        vmem((8, 2, 2, HALF, 128), BF16),
        vmem((8, 2, 2, HALF, 128), BF16),
        vmem((8, 2, 2, HALF, 128), BF16),
        vmem((nx, 2, HALF, 512), BF16),
        vmem((nx, 2, HALF, 512), BF16),
        vmem((2, TOK, 2048), BF16),
        vmem((TOK, 128), F32),
        vmem((8, TOK), F32),
        vmem((4, 8, TOK), F32),
        vmem((4, 2, TOK, 128), BF16),
        vmem((2, 4, TOK, 128), BF16),
        vmem((TOK, 128), F32),
        vmem((2, TOK, 128), BF16),
        pltpu.SemaphoreType.DMA((N_SEND,)),
        pltpu.SemaphoreType.DMA((RECV.total,)),
        pltpu.SemaphoreType.DMA((LOCAL.total,)),
        pltpu.SemaphoreType.REGULAR((4,)),
    ]
    any_spec = pl.BlockSpec(memory_space=pl.ANY)
    out_shape = (
        jax.ShapeDtypeStruct((2, TOK, 128), BF16),
        jax.ShapeDtypeStruct((2, 256, 128), F32),
        jax.ShapeDtypeStruct((2, 256, 128), F32),
    )
    outs = pl.pallas_call(
        kernel,
        out_shape=out_shape,
        in_specs=[any_spec] * 7,
        out_specs=(any_spec,) * 3,
        scratch_shapes=scratch,
        compiler_params=pltpu.CompilerParams(
            collective_id=0, has_side_effects=True, vmem_limit_bytes=60 * 2**20
        ),
        cost_estimate=pl.CostEstimate(flops=2 * 768 * 1024 * 1024, bytes_accessed=13 * 2**20, transcendentals=0),
        name="outer_step",
    )(
        delta_codes.reshape(2, 32, 2, 64, 128),
        scale_exponents.reshape(2, 32, 8, 128),
        outer_params,
        outer_momentum,
        tensor_partials.reshape(TOK, D),
        residual_stream,
        norm_gain.reshape(64, 128),
    )
    return pl.pallas_call(
        hand_over,
        out_shape=out_shape,
        in_specs=[any_spec] * 3,
        out_specs=(any_spec,) * 3,
        scratch_shapes=[vmem(out.shape, out.dtype) for out in out_shape] + [pltpu.SemaphoreType.DMA((6,))],
        name="hand_over",
    )(*outs)


def solution(mesh):
    return jax.shard_map(
        per_device,
        mesh=mesh,
        in_specs=(
            P("replica", None, None, "tensor"),
            P("replica", None, None, "tensor"),
            P(None, "replica", "tensor"),
            P(None, "replica", "tensor"),
            P("tensor", "replica", None),
            P("replica", "tensor"),
            P(),
        ),
        out_specs=(
            P(None, "replica", "tensor"),
            P(None, "replica", "tensor"),
            P(None, "replica", "tensor"),
        ),
        check_vma=False,
    )
```

```python
import jax
import jax.numpy as jnp
from jax import lax
from jax.experimental import pallas as pl
from jax.experimental.pallas import tpu as pltpu
from jax.sharding import PartitionSpec as P

D = 8192
TOK = 384
MESH = pl.DeviceIdType.MESH
F32 = jnp.float32
BF16 = jnp.bfloat16

outer_rate = 0.7
outer_beta = 0.9
norm_epsilon = 1e-05

Y_FIRST = (0, 1, 2, 4, 5, 6, 7)
X_FIRST = (3,)
H_ORDER = (0, 3, 1, 2, 4, 5, 6, 7)
HALF = TOK // 2

PLAN = {
    "other": (1.5, 3.7, 6.8, 10.0),
    "own": (3.0, 5.4, 7.5, 10.7),
    "pair": (4.9, 6.3, 9.6, 13.0),
    "hop": 3.0,
    "cross": 4.2,
    "greet": (6.0, 8.0, 10.0, 11.0),
    "gather": (23.2, 29.7),
    "piece": 0.9,
    "relay": 4.0,
    "start": (3.1, 3.2, 6.5, 10.5, 15.2, 19.9, 24.6, 29.3),
    "y": (0.0, 8.0, 16.0, 23.0),
    "x": (0.0, 11.0, 18.0, 24.0, 29.0),
    "squares": 8.0,
}


class Slots:
    def __init__(self):
        self.total = 0
        self.base = {}

    def add(self, name, count):
        self.base[name] = self.total
        self.total += count

    def __getitem__(self, name):
        return self.base[name]


RECV = Slots()
for _name, _count in (
    ("sib", 4), ("z", 4 * 2 * 4), ("xh", 4), ("a2a", 8), ("ag", 4 * 2 * 4), ("ya", 8 * 2), ("yb", 8 * 2),
    ("yc", 8 * 2), ("xl", 8 * 2), ("asib", 8), ("ss", 4), ("p", 16),
):
    RECV.add(_name, _count)
N_SEND = 256
LOCAL = Slots()
for _name, _count in (("codes", 4), ("part", 8), ("misc", 5), ("out", 9)):
    LOCAL.add(_name, _count)


def decode_nibble(code):
    magnitude = jnp.bitwise_and(code, 7).astype(F32)
    value = jnp.maximum(jnp.maximum(0.5 * magnitude, magnitude - 2.0), 2.0 * magnitude - 8.0)
    return jnp.where(code >= 8, -value, value)


def kernel(
    codes, exps, params, momentum, partials, residual, gain,
    kv_out, params_out, momentum_out,
    cbuf, ebuf, pbuf, mbuf, rbuf, gbuf,
    dec, sibr, zrecv, zout, fin, xout, xrecv, grad, newp, newm, frag, wbuf,
    part, yra, yrb, yrc, yout, xo, xr, xr4, xs, abuf, ssacc, ssout, ssr, pout, precv, invb, kvbuf,
    ssem, rsem, lsem, plane,
):
    r = lax.axis_index("replica")
    t = lax.axis_index("tensor")
    xh = r // 16
    z = lax.rem(r // 2, 8)
    c = lax.rem(r, 2)
    xl = t // 4
    y = lax.rem(t, 4)

    def dev(xh_, z_, c_, xl_, y_):
        return (xh_ * 16 + z_ * 2 + c_, xl_ * 4 + y_)

    def zp(n):
        return lax.rem(z + 8 + n, 8)

    def yp(n):
        return lax.rem(y + 4 + n, 4)

    sibling = dev(xh, z, 1 - c, xl, y)
    x_pair = dev(xh, z, c, 1 - xl, y)
    x_cross = dev(1 - xh, z, c, 1 - xl, y)
    xh_pair = dev(1 - xh, z, c, xl, y)
    z_next = (dev(xh, zp(1), c, xl, y), dev(xh, zp(-1), c, xl, y))
    y_next = (dev(xh, z, c, xl, yp(1)), dev(xh, z, c, xl, yp(-1)))

    sends = []

    def send(src, dst, recv_index, device, cond=None, inside=None, like=None):
        index = len(sends)
        copy = pltpu.make_async_remote_copy(
            src_ref=src, dst_ref=dst, send_sem=ssem.at[index], recv_sem=rsem.at[recv_index],
            device_id=device, device_id_type=MESH,
        )
        if cond is None:
            copy.start()
        else:
            pl.when(cond)(copy.start)
        sends.append((src if like is None else like, cond if inside is None else inside))

    def wait_send(index):
        like, cond = sends[index]
        copy = pltpu.make_async_remote_copy(
            src_ref=like, dst_ref=like, send_sem=ssem.at[index], recv_sem=rsem.at[0],
            device_id=sibling, device_id_type=MESH,
        )
        if cond is None:
            copy.wait_send()
        else:
            pl.when(cond)(copy.wait_send)

    def wait_recv(dst, recv_index):
        pltpu.make_async_remote_copy(
            src_ref=dst, dst_ref=dst, send_sem=ssem.at[0], recv_sem=rsem.at[recv_index],
            device_id=sibling, device_id_type=MESH,
        ).wait_recv()

    def load(src, dst, index):
        copy = pltpu.make_async_copy(src, dst, lsem.at[index])
        copy.start()
        return copy

    code_loads = [None] * 4
    part_loads = [None] * 8

    def load_codes(q):
        code_loads[q] = load(codes.at[q // 2, :, q % 2], cbuf.at[q], LOCAL["codes"] + q)

    def load_part(k):
        part_loads[k] = load(partials.at[:, pl.ds(1024 * k, 1024)], part.at[k], LOCAL["part"] + k)

    load_codes(0)
    exp_load = load(exps, ebuf, LOCAL["misc"])
    res_load = load(residual, rbuf, LOCAL["misc"] + 1)
    first = [2 * (H_ORDER[0] % 4), 2 * (H_ORDER[0] % 4) + 1]
    for k in first:
        load_part(k)
    state_loads = []

    def more_loads():
        load_codes(1)
        rest = [k for u in H_ORDER for k in (2 * (u % 4), 2 * (u % 4) + 1) if u < 4 and k not in first]
        for k in rest[:2]:
            load_part(k)
        load_codes(2)
        load_codes(3)
        for k in rest[2:]:
            load_part(k)
        state_loads.append(load(gain, gbuf, LOCAL["misc"] + 4))
        state_loads.append(load(params, pbuf, LOCAL["misc"] + 2))
        state_loads.append(load(momentum, mbuf, LOCAL["misc"] + 3))

    barrier = pltpu.get_barrier_semaphore()
    for other in (sibling, x_pair, x_cross) + y_next + z_next:
        pl.semaphore_signal(barrier, inc=1, device_id=other, device_id_type=MESH)

    def greet(stage):
        others = (y_next, (x_pair, x_cross), (x_pair, x_cross), (sibling,))
        if stage:
            pl.semaphore_wait(plane.at[stage - 1], len(others[stage - 1]))
        if stage < 4:
            for other in others[stage]:
                pl.semaphore_signal(plane.at[stage], inc=1, device_id=other, device_id_type=MESH)

    def decode(q, core):
        j, half = q // 2, q % 2

        @pl.loop(0, 16)
        def _(i):
            owner = i * 2 + core
            for b in range(4):
                exponent = ebuf[j, owner, pl.ds(4 * half + b, 1), :]
                scale = jnp.left_shift(jnp.ones_like(exponent), exponent + 5).astype(F32) * 2.0**-5
                words = cbuf[q, owner, pl.ds(16 * b, 16), :]
                low = decode_nibble(jnp.bitwise_and(words, 15)) * scale
                high = decode_nibble(jnp.bitwise_and(jnp.right_shift(words, 4), 15)) * scale
                dec[q, core, i // 8, lax.rem(i, 8), pl.ds(16 * b, 16), :] = low.astype(BF16)
                dec[q, core, i // 8, lax.rem(i, 8), pl.ds(64 + 16 * b, 16), :] = high.astype(BF16)

    tasks = []

    def task(time, function, *arguments):
        tasks.append((time, len(tasks), function, arguments))

    def g_decode_other(q):
        code_loads[q].wait()
        if q == 0:
            exp_load.wait()
        decode(q, 1 - c)
        if q == 0:
            pl.semaphore_wait(barrier, 7)
            greet(0)
            more_loads()
        send(dec.at[q, 1 - c], sibr.at[q], RECV["sib"] + q, sibling)

    def g_decode_own(q):
        decode(q, c)

    def g_pair(q):
        wait_recv(sibr.at[q], RECV["sib"] + q)

        @pl.loop(0, 16)
        def _(i):
            a, b = i // 8, lax.rem(i, 8)
            dec[q, c, a, b] = (dec[q, c, a, b].astype(F32) + sibr[q, a, b].astype(F32)).astype(BF16)

        for d in range(2):
            send(dec.at[q, c, d, zp(4)], zrecv.at[q, d, 0, d], RECV["z"] + (q * 2 + d) * 4, z_next[d])

    def g_ring(q, step):
        for d in range(2):
            sign = 1 - 2 * d
            target = zp(sign * (5 - step))
            index = RECV["z"] + (q * 2 + d) * 4 + step - 2
            if step == 2:
                wait_recv(zrecv.at[q, d, 0, d], index)
                zout[q, d, step - 2, d] = (
                    dec[q, c, d, target].astype(F32) + zrecv[q, d, 0, d].astype(F32)
                ).astype(BF16)
                zout[q, d, step - 2, 1 - d] = dec[q, c, 1 - d, target]
            else:
                wait_recv(zrecv.at[q, d, step - 2], index)
                for a in range(2):
                    zout[q, d, step - 2, a] = (
                        dec[q, c, a, target].astype(F32) + zrecv[q, d, step - 2, a].astype(F32)
                    ).astype(BF16)
            send(zout.at[q, d, step - 2], zrecv.at[q, d, step - 1], index + 1, z_next[d])

    def g_final(q):
        for d in range(2):
            wait_recv(zrecv.at[q, d, 3], RECV["z"] + (q * 2 + d) * 4 + 3)

        def total(a):
            return (
                dec[q, c, a, z].astype(F32) + zrecv[q, 0, 3, a].astype(F32) + zrecv[q, 1, 3, a].astype(F32)
            )

        xout[q] = total(1 - xh).astype(BF16)
        send(xout.at[q], xrecv.at[q], RECV["xh"] + q, xh_pair)
        fin[q] = total(xh)

    away = (1, 3, 2, 0)

    def place_of(delta):
        return jnp.where(delta == 1, 0, jnp.where(delta == 3, 1, jnp.where(delta == 2, 2, 3)))

    def g_update(q):
        j, half = q // 2, q % 2
        if q == 0:
            state_loads[1].wait()
            state_loads[2].wait()
        wait_recv(xrecv.at[q], RECV["xh"] + q)
        summed = fin[q] + xrecv[q].astype(F32)
        grad[q, pl.ds(0, 64, stride=2), :] = summed[:64]
        grad[q, pl.ds(1, 64, stride=2), :] = summed[64:]
        outer_grad = grad[q] * (1.0 / 32.0)
        rows = pl.ds(128 * half, 128)
        new_momentum = outer_beta * mbuf[j, rows, :] + outer_grad
        new_params = pbuf[j, rows, :] - outer_rate * (outer_grad + outer_beta * new_momentum)
        newm[j, rows, :] = new_momentum
        newp[j, rows, :] = new_params
        frag[q] = new_params.astype(BF16)
        y_to = 2 * c + half
        column = place_of(lax.rem(y - y_to + 4, 4))
        slot = wbuf.at[xh, z, :, pl.ds(pl.multiple_of(128 * column, 128), 128)]
        index = RECV["a2a"] + xh * 4 + column
        here = (c == j) & (y == y_to)

        @pl.when(here)
        def _():
            pltpu.make_async_copy(frag.at[q], slot, rsem.at[index]).start()

        send(frag.at[q], slot, index, dev(xh, z, j, xl, y_to), jnp.logical_not(here))
        send(frag.at[q], slot, index, dev(1 - xh, z, j, xl, y_to))

    def w_block(source_z, i):
        return wbuf.at[:, source_z, :, pl.ds(128 * i, 128)]

    def w_half(source_z, a, i):
        return wbuf.at[a, source_z, :, pl.ds(128 * i, 128)]

    def w_step(i, core, step):
        like = w_block(0, i) if step < 3 else w_half(0, 0, i)
        mine = c == core

        @pl.when(mine)
        def _():
            if step == 0:
                for a in range(2):
                    wait_recv(w_half(z, a, i), RECV["a2a"] + a * 4 + i)
            for d in range(2):
                index = RECV["ag"] + (i * 2 + d) * 4 + step
                origin = zp((2 * d - 1) * step)
                if 0 < step < 4:
                    wait_recv(w_block(origin, i), index - 1)
                if step < 3:
                    send(w_block(origin, i), w_block(origin, i), index, z_next[d], inside=mine, like=like)
                elif step == 3:
                    piece = w_half(origin, d, i)
                    send(piece, piece, index, z_next[d], inside=mine, like=like)
                else:
                    wait_recv(w_half(origin, d, i), index - 1)

    def lanes(x_, y_):
        return pl.ds(pl.multiple_of(128 * (x_ * 4 + y_), 128), 128)

    def add_rows(out, *terms):
        for g in range(2):
            @pl.loop(0, HALF // 64)
            def _(i):
                at = pl.multiple_of(i * 64, 64)
                value = terms[0](g, at).astype(F32)
                for term in terms[1:]:
                    value = value + term(g, at).astype(F32)
                out(g, at, value)

    def rows(at):
        return pl.ds(at, 64)

    def tokens(u):
        return pl.ds(HALF * (u // 4), HALF)

    def groups(u):
        return pl.ds(2 * (u % 4), 2)

    def part_term(u, own):
        return lambda g, at: part[2 * (u % 4) + g, pl.ds(HALF * (u // 4) + at, 64), own]

    loaded = []

    def h_load(u):
        if u % 4 in loaded:
            return
        loaded.append(u % 4)
        for k in (2 * (u % 4), 2 * (u % 4) + 1):
            part_loads[k].wait()
            if len(loaded) == 1 and k % 2 == 0:
                res_load.wait()

            @pl.when(t == k)
            def _():
                @pl.loop(0, TOK // 16)
                def _(i):
                    at = pl.ds(pl.multiple_of(i * 16, 16), 16)
                    part[k, at, :] = (part[k, at, :].astype(F32) + rbuf[at, :].astype(F32)).astype(BF16)

    def hy_start(u):
        h_load(u)
        for d in range(2):
            send(part.at[groups(u), tokens(u), lanes(d, yp(2))], yra.at[u, d], RECV["ya"] + u * 2 + d, y_next[d])
        for d in range(2):
            piece = part.at[groups(u), tokens(u), lanes(1 - d, yp(1 - 2 * d))]
            send(piece, yrb.at[u, d], RECV["yb"] + u * 2 + d, y_next[d])

    def hy_middle(u):
        for d in range(2):
            wait_recv(yra.at[u, d], RECV["ya"] + u * 2 + d)

            def put(g, at, value, d=d):
                yout[u, d, g, rows(at), :] = value.astype(BF16)

            add_rows(put, part_term(u, lanes(d, yp(1 - 2 * d))), lambda g, at, d=d: yra[u, d, g, rows(at), :])
            send(yout.at[u, d], yrc.at[u, d], RECV["yc"] + u * 2 + d, y_next[d])

    def hy_cross(u):
        for d in range(2):
            wait_recv(yrb.at[u, d], RECV["yb"] + u * 2 + d)
            wait_recv(yrc.at[u, d], RECV["yc"] + u * 2 + d)

        for x_ in range(2):
            def put(g, at, value, x_=x_):
                xo[u, x_, g, rows(at), :] = value.astype(BF16)

            add_rows(
                put, part_term(u, lanes(x_, y)), lambda g, at, x_=x_: yrb[u, 1 - x_, g, rows(at), :],
                lambda g, at, x_=x_: yrc[u, x_, g, rows(at), :],
            )
            send(xo.at[u, x_], xr.at[u, x_], RECV["xl"] + u * 2 + x_, x_pair)

    def finish(u, x_, g, at, value):
        k = 2 * (u % 4) + g
        hidden = value.astype(BF16).astype(F32)
        scaled = hidden * gbuf[pl.ds(8 * k + 4 * x_ + y, 1), :]
        to = pl.ds(HALF * (u // 4) + at, 64)
        abuf[c, to, pl.ds(pl.multiple_of(128 * (2 * k + x_), 128), 128)] = scaled.astype(BF16)
        ssacc[to, :] += hidden * hidden

    def unit_share(core, u):
        return abuf.at[core, tokens(u), pl.ds(512 * (u % 4), 512)]

    def finished(u):
        send(unit_share(c, u), unit_share(c, u), RECV["asib"] + u, sibling)

    gain_waited = []

    def gain_ready():
        if not gain_waited:
            state_loads[0].wait()
            ssacc[...] = jnp.zeros_like(ssacc)
            gain_waited.append(True)

    def hy_end(u):
        gain_ready()
        for x_ in range(2):
            wait_recv(xr.at[u, x_], RECV["xl"] + u * 2 + x_)
            add_rows(
                lambda g, at, value, x_=x_: finish(u, x_, g, at, value),
                lambda g, at, x_=x_: xo[u, x_, g, rows(at), :], lambda g, at, x_=x_: xr[u, x_, g, rows(at), :],
            )
        finished(u)

    def hx_start(u):
        h_load(u)
        other = pl.ds(pl.multiple_of(512 * (1 - xl), 512), 512)
        send(part.at[groups(u), tokens(u), other], xr4.at[X_FIRST.index(u)], RECV["xl"] + u * 2, x_pair)

    def hx_lanes(y_):
        return pl.ds(pl.multiple_of(128 * y_, 128), 128)

    def hx_cross(u):
        n = X_FIRST.index(u)
        wait_recv(xr4.at[n], RECV["xl"] + u * 2)
        own = pl.ds(pl.multiple_of(512 * xl, 512), 512)

        def put(g, at, value):
            xs[n, g, rows(at), :] = value.astype(BF16)

        add_rows(put, part_term(u, own), lambda g, at: xr4[n, g, rows(at), :])
        for d in range(2):
            send(xs.at[n, d, :, hx_lanes(yp(2))], yra.at[u, d, 0], RECV["ya"] + u * 2 + d, y_next[d])

    def hx_middle(u):
        n = X_FIRST.index(u)
        for d in range(2):
            wait_recv(yra.at[u, d, 0], RECV["ya"] + u * 2 + d)
            own = hx_lanes(yp(1 - 2 * d))

            @pl.loop(0, HALF // 64)
            def _(i, d=d, own=own):
                at = rows(pl.multiple_of(i * 64, 64))
                xs[n, d, at, own] = (xs[n, d, at, own].astype(F32) + yra[u, d, 0, at, :].astype(F32)).astype(BF16)

            send(xs.at[n, :, :, own], yrc.at[u, d], RECV["yc"] + u * 2 + d, y_next[d])

    def hx_end(u):
        n = X_FIRST.index(u)
        gain_ready()
        for d in range(2):
            wait_recv(yrc.at[u, d], RECV["yc"] + u * 2 + d)
        own = hx_lanes(y)

        def put(g, at, value):
            xo[u, 0, g, rows(at), :] = value.astype(BF16)
            finish(u, xl, g, at, value)

        add_rows(
            put, lambda g, at: xs[n, g, rows(at), own], lambda g, at: yrc[u, 0, g, rows(at), :],
            lambda g, at: yrc[u, 1, g, rows(at), :],
        )
        send(xo.at[u, 0], xr.at[u, 0], RECV["xl"] + u * 2 + 1, x_pair)

    def hx_last(u):
        wait_recv(xr.at[u, 0], RECV["xl"] + u * 2 + 1)
        add_rows(
            lambda g, at, value: finish(u, 1 - xl, g, at, value), lambda g, at: xr[u, 0, g, rows(at), :]
        )
        finished(u)

    def ss_send():
        for b in range(3):
            block = jnp.sum(ssacc[pl.ds(128 * b, 128), :].T, axis=0, keepdims=True)
            ssout[:, pl.ds(128 * b, 128)] = jnp.broadcast_to(block, (8, 128))
        ssr[y] = ssout[...]
        for e in range(1, 4):
            send(ssout, ssr.at[y], RECV["ss"] + y, dev(xh, z, c, xl, yp(e)))

    def ss_receive():
        for e in range(1, 4):
            wait_recv(ssr.at[yp(e)], RECV["ss"] + yp(e))
        total = ssr[0] + ssr[1] + ssr[2] + ssr[3]
        inverse = lax.rsqrt(total * (1.0 / D) + norm_epsilon) * D**-0.5
        for b in range(3):
            block = jnp.broadcast_to(inverse[0:1, 128 * b : 128 * b + 128], (128, 128))
            invb[pl.ds(128 * b, 128), :] = block.T

    def hidden_ready(th):
        for u in range(4 * th, 4 * th + 4):
            wait_recv(unit_share(1 - c, u), RECV["asib"] + u)

    pout_like = pout.at[0, 0, pl.ds(0, HALF)]

    def project(i, core, th):
        mine = c == core
        at = pl.ds(HALF * th, HALF)

        @pl.when(mine)
        def _():
            w = wbuf[:, :, :, pl.ds(128 * i, 128)].reshape(2048, 128)
            a = abuf[:, at, :].reshape(2 * HALF, 2048)
            products = jnp.dot(a, w, preferred_element_type=F32).astype(BF16)
            for b in range(2):
                pout[i, b, at, :] = products[b * HALF : b * HALF + HALF]
            for b in range(2):
                piece = pout.at[i, b, at]
                slot = precv.at[core, y, at]
                index = RECV["p"] + (core * 4 + y) * 2 + th
                if away[i] == 0 and b == core:
                    pltpu.make_async_copy(piece, slot, rsem.at[index]).start()
                else:
                    device = dev(xh, z, b, xl, yp(away[i]))
                    send(piece, slot, index, device, inside=mine, like=pout_like)

    def result(th):
        for j in range(2):
            for source in range(4):
                wait_recv(precv.at[j, source, pl.ds(HALF * th, HALF)], RECV["p"] + (j * 4 + source) * 2 + th)

            @pl.loop(0, HALF // 32)
            def _(i):
                at = pl.ds(pl.multiple_of(HALF * th + i * 32, 32), 32)
                value = precv[j, 0, at, :].astype(F32)
                for source in range(1, 4):
                    value = value + precv[j, source, at, :].astype(F32)
                kvbuf[j, at, :] = (value * invb[at, :]).astype(BF16)

    for q in range(4):
        task(PLAN["other"][q], g_decode_other, q)
        task(PLAN["own"][q], g_decode_own, q)
        base = PLAN["pair"][q]
        task(base, g_pair, q)
        for step in (2, 3, 4):
            task(base + PLAN["hop"] * (step - 1), g_ring, q, step)
        task(base + PLAN["hop"] * 4, g_final, q)
        task(base + PLAN["hop"] * 4 + PLAN["cross"], g_update, q)
        task(PLAN["greet"][q], greet, q + 1)
    ready = [0.0, 0.0]
    for n, u in enumerate(H_ORDER):
        start = PLAN["start"][n]
        if u in Y_FIRST:
            steps = zip((hy_start, hy_middle, hy_cross, hy_end), PLAN["y"])
        else:
            steps = zip((hx_start, hx_cross, hx_middle, hx_end, hx_last), PLAN["x"])
        for function, after in steps:
            task(start + after, function, u)
            ready[u // 4] = max(ready[u // 4], start + after)
    ready[1] = max(ready) + 0.01
    for th in range(2):
        task(ready[th] + 0.5, hidden_ready, th)
    task(ready[1] + 0.3, ss_send)
    for core in range(2):
        for i in range(4):
            base = PLAN["gather"][core] + PLAN["piece"] * i
            for step in range(5):
                task(base + PLAN["relay"] * step, w_step, i, core, step)
            for th in range(2):
                task(max(base + PLAN["relay"] * 4, ready[th] + 0.5) + 0.1, project, i, core, th)
    end = max(item[0] for item in tasks)
    task(ready[1] + PLAN["squares"], ss_receive)
    task(max(end, ready[1] + PLAN["squares"]) + 1.0, result, 0)
    task(max(end, ready[1] + PLAN["squares"]) + 2.0, result, 1)
    outs = []
    drained = 0

    def drain(limit, most):
        count = max(0, min(most, limit - drained))
        for index in range(drained, drained + count):
            wait_send(index)
        return drained + count

    for _, _, function, arguments in sorted(tasks, key=lambda item: item[:2]):
        if function is result and arguments == (0,):
            drained = drain(len(sends) - 16, len(sends))
        function(*arguments)
        if function is g_update and arguments == (3,):
            outs.append(load(newp, params_out, LOCAL["out"]))
            outs.append(load(newm, momentum_out, LOCAL["out"] + 1))
        if function is result:
            half = pl.ds(HALF * arguments[0], HALF)
            outs.append(load(kvbuf.at[:, half], kv_out.at[:, half], LOCAL["out"] + 2 + arguments[0]))
        else:
            drained = drain(len(sends) - 48, 6)
    drained = drain(len(sends), len(sends))
    for copy in outs:
        copy.wait()


def hand_over(*refs):
    ins, outs, held, sems = refs[:3], refs[3:6], refs[6:9], refs[9]
    loads = [pltpu.make_async_copy(ins[n], held[n], sems.at[n]) for n in range(3)]
    stores = [pltpu.make_async_copy(held[n], outs[n], sems.at[3 + n]) for n in range(3)]
    for copy in loads:
        copy.start()
    for load, store in zip(loads, stores):
        load.wait()
        store.start()
    for copy in stores:
        copy.wait()


def per_device(
    delta_codes, scale_exponents, outer_params, outer_momentum, tensor_partials, residual_stream, norm_gain
):
    nx = max(len(X_FIRST), 1)
    vmem = pltpu.VMEM
    scratch = [
        vmem((4, 32, 64, 128), jnp.int32),
        vmem((2, 32, 8, 128), jnp.int32),
        vmem((2, 256, 128), F32),
        vmem((2, 256, 128), F32),
        vmem((TOK, 1024), BF16),
        vmem((64, 128), F32),
        vmem((4, 2, 2, 8, 128, 128), BF16),
        vmem((4, 2, 8, 128, 128), BF16),
        vmem((4, 2, 4, 2, 128, 128), BF16),
        vmem((4, 2, 3, 2, 128, 128), BF16),
        vmem((4, 128, 128), F32),
        vmem((4, 128, 128), BF16),
        vmem((4, 128, 128), BF16),
        vmem((4, 128, 128), F32),
        vmem((2, 256, 128), F32),
        vmem((2, 256, 128), F32),
        vmem((4, 128, 128), BF16),
        vmem((2, 8, 128, 512), BF16),
        vmem((8, TOK, 1024), BF16),
        vmem((8, 2, 2, HALF, 128), BF16),
        vmem((8, 2, 2, HALF, 128), BF16),
        vmem((8, 2, 2, HALF, 128), BF16),
        vmem((8, 2, 2, HALF, 128), BF16),
        vmem((8, 2, 2, HALF, 128), BF16),
        vmem((8, 2, 2, HALF, 128), BF16),
        vmem((nx, 2, HALF, 512), BF16),
        vmem((nx, 2, HALF, 512), BF16),
        vmem((2, TOK, 2048), BF16),
        vmem((TOK, 128), F32),
        vmem((8, TOK), F32),
        vmem((4, 8, TOK), F32),
        vmem((4, 2, TOK, 128), BF16),
        vmem((2, 4, TOK, 128), BF16),
        vmem((TOK, 128), F32),
        vmem((2, TOK, 128), BF16),
        pltpu.SemaphoreType.DMA((N_SEND,)),
        pltpu.SemaphoreType.DMA((RECV.total,)),
        pltpu.SemaphoreType.DMA((LOCAL.total,)),
        pltpu.SemaphoreType.REGULAR((4,)),
    ]
    any_spec = pl.BlockSpec(memory_space=pl.ANY)
    out_shape = (
        jax.ShapeDtypeStruct((2, TOK, 128), BF16),
        jax.ShapeDtypeStruct((2, 256, 128), F32),
        jax.ShapeDtypeStruct((2, 256, 128), F32),
    )
    outs = pl.pallas_call(
        kernel,
        out_shape=out_shape,
        in_specs=[any_spec] * 7,
        out_specs=(any_spec,) * 3,
        scratch_shapes=scratch,
        compiler_params=pltpu.CompilerParams(
            collective_id=0, has_side_effects=True, vmem_limit_bytes=60 * 2**20
        ),
        cost_estimate=pl.CostEstimate(flops=2 * 768 * 1024 * 1024, bytes_accessed=13 * 2**20, transcendentals=0),
        name="outer_step",
    )(
        delta_codes.reshape(2, 32, 2, 64, 128),
        scale_exponents.reshape(2, 32, 8, 128),
        outer_params,
        outer_momentum,
        tensor_partials.reshape(TOK, D),
        residual_stream,
        norm_gain.reshape(64, 128),
    )
    return pl.pallas_call(
        hand_over,
        out_shape=out_shape,
        in_specs=[any_spec] * 3,
        out_specs=(any_spec,) * 3,
        scratch_shapes=[vmem(out.shape, out.dtype) for out in out_shape] + [pltpu.SemaphoreType.DMA((6,))],
        name="hand_over",
    )(*outs)


def solution(mesh):
    return jax.shard_map(
        per_device,
        mesh=mesh,
        in_specs=(
            P("replica", None, None, "tensor"),
            P("replica", None, None, "tensor"),
            P(None, "replica", "tensor"),
            P(None, "replica", "tensor"),
            P("tensor", "replica", None),
            P("replica", "tensor"),
            P(),
        ),
        out_specs=(
            P(None, "replica", "tensor"),
            P(None, "replica", "tensor"),
            P(None, "replica", "tensor"),
        ),
        check_vma=False,
    )
```
